256 devices in a mesh: resp: 8 (over x, core), seq: 32 (over y, z).
Axes of the slice: x: 4, y: 4, z: 8, core: 2. Of those that a mesh axis runs over, the one named last changes fastest.
Arguments:
- queries: bfloat16 [8, 4096, 4096], P('resp', 'seq'), may hold values from -10 to 10
- resp_keys: bfloat16 [8, 4096, 512], P('resp', 'seq'), may hold values from -10 to 10
- response_values: bfloat16 [8, 4096, 512], P('resp', 'seq'), may hold values from -6 to 6
- prompt_keys: bfloat16 [2048, 512], P(('resp', 'seq')), may hold values from -10 to 10
- shared_prompt_values: bfloat16 [2048, 512], P(('resp', 'seq')), may hold values from -6 to 6
- value_head: float32 [4096], replicated, may hold values from -0.09375 to 0.09375
- token_ids: int32 [8, 4096], P('resp', 'seq'), may hold values from 0 to 128255
- policy_logprobs: float32 [8, 4096], P('resp', 'seq'), may hold values from -10 to -0.5
- ref_table: float32 [128256], replicated, may hold values from -10 to -0.5
- scores: float32 [8], P('resp'), may hold values from -4 to 4
- lengths: int32 [8], P('resp'), may hold values from 1 to 4096, 20480 in all
- horizon: float32 [8], P('resp'), may hold values from 40 to 16384
Outputs:
- attn_out: bfloat16 [8, 4096, 4096], P('resp', 'seq')
- values: float32 [8, 4096], P('resp', 'seq')
- advantages: float32 [8, 4096], P('resp', 'seq')
The draws below stay inside these ranges and needn't reach their ends.
Inputs may be any that keep to these rules, and one draw needn't show every extreme that they name: `lengths`: each response's valid positions; the longest response fills all 4096.
All inputs are finite; a program needn't handle non-finite values. No bound on the sum of `lengths` on one device may be relied on, other than what follows from the above.
Results may differ from the reference program's by a relative error of at most 0.012.
Values may be sent and summed in bfloat16 or wider, within the bound.
A program may use at most 192 MiB of HBM per device.

```python
import math
import jax
import jax.numpy as jnp
import numpy as np
from jax import lax

QUERY_HEAD_COUNT = 32
KEY_VALUE_HEADS = 4
HEAD_SIZE = 128
VOCAB = 128256
RESPONSE_COUNT = 8
RESPONSE_LENGTH = 4096
PROMPT_LENGTH = 2048


def draw_queries(key, part):
    key = jax.random.fold_in(key, 101)
    joined_dimensions = (RESPONSE_COUNT, RESPONSE_LENGTH, QUERY_HEAD_COUNT * HEAD_SIZE)
    backdrop = jnp.clip(1.5 * jax.random.normal(key, joined_dimensions, jnp.float32), -8.0, 8.0)
    return backdrop.astype(jnp.bfloat16)


def draw_prompt_keys(key, part):
    key = jax.random.fold_in(key, 202)
    joined_dimensions = (PROMPT_LENGTH, KEY_VALUE_HEADS * HEAD_SIZE)
    backdrop = jnp.clip(2.0 * jax.random.normal(key, joined_dimensions, jnp.float32), -8.0, 8.0)
    return backdrop.astype(jnp.bfloat16)


def draw_resp_keys(key, part):
    key = jax.random.fold_in(key, 303)
    joined_dimensions = (RESPONSE_COUNT, RESPONSE_LENGTH, KEY_VALUE_HEADS * HEAD_SIZE)
    backdrop = jnp.clip(2.0 * jax.random.normal(key, joined_dimensions, jnp.float32), -8.0, 8.0)
    return backdrop.astype(jnp.bfloat16)


def set_ends(values, key, least, high):
    spot = [jax.random.randint(jax.random.fold_in(key, axis), (), 0, length) for axis, length in enumerate(values.shape)]
    longest = values.shape.index(max(values.shape))
    next_to = spot[:longest] + [(spot[longest] + 1) % values.shape[longest]] + spot[longest + 1:]
    return values.at[tuple(spot)].set(least).at[tuple(next_to)].set(high)


def level_of(stream_key, extent, shards, low, largest):
    gain = 1.0
    for position, shards_of in shards:
        draws = jax.random.uniform(jax.random.fold_in(jax.random.fold_in(stream_key, 6), position), (shards_of,), jnp.float32, low / len(shards), largest / len(shards))
        gain = gain * jnp.repeat(jnp.exp(draws), extent[position] // shards_of).reshape((-1,) + (1,) * (len(extent) - 1 - position))
    return gain


def skewed_wide(stream_key, dims, number_of, lean):
    weights = [min(1 << octave, number_of + 1 - (1 << octave)) * (1 << 20) // math.isqrt((1 << octave) ** lean) + 1 for octave in range((number_of + 1).bit_length()) if 1 << octave <= number_of]
    spread = 1 + sum(weights) // (1 << 30)
    grid = np.cumsum(np.array([max(1, weight // spread) for weight in weights]))
    pick = jax.random.randint(jax.random.fold_in(stream_key, 1), dims, 0, int(grid[len(weights) - 1]))
    start = jnp.left_shift(1, jnp.searchsorted(jnp.asarray(grid, jnp.int32), pick, side="right").astype(jnp.int32))
    rank = start - 1 + jax.random.randint(jax.random.fold_in(stream_key, 4), dims, 0, 1 << 30) % jnp.minimum(start, number_of + 1 - start)
    return jax.random.permutation(jax.random.fold_in(stream_key, 2), number_of)[rank].astype(jnp.int32)


def split_up(count, total, reach, lean):
    loads = [(1 << 20) // math.isqrt(grade ** lean) + 1 for grade in range(2, count + 1)]
    surplus, holding = total - reach - (count - 1), [1] * (count - 1)
    while surplus > 0:
        movable = [i for i in range(count - 1) if holding[i] < reach]
        pool, remaining = sum([loads[i] for i in movable]), surplus
        for i in movable:
            addition = min(reach - holding[i], max(1, remaining * loads[i] // pool), surplus)
            holding[i] = holding[i] + addition
            surplus = surplus - addition
    return np.array([reach] + holding)


def uneven_parts(rng, amount, total, bound, slope):
    if amount == 2:
        one = jax.random.randint(rng, (), max(1, total - bound), min(bound, total - 1) + 1)
        return jnp.stack([one, total - one])
    sizes = jnp.asarray(split_up(amount, total, bound, slope), jnp.int32)
    twos = (amount - 1) // 2
    giver, receiver = sizes[1:1 + 2 * twos:2], sizes[2:2 + 2 * twos:2]
    slack = jnp.minimum(giver - 1, bound - receiver)
    passed = jax.random.randint(jax.random.fold_in(rng, 1), (twos,), 0, 1 << 20) % (slack + 1)
    sizes = sizes.at[1:1 + 2 * twos:2].set(giver - passed).at[2:2 + 2 * twos:2].set(receiver + passed)
    return sizes[jax.random.permutation(jax.random.fold_in(rng, 2), amount)]


def normal_values(stream_key, extent, scale, limit, split=(), kind=jnp.bfloat16):
    factor_of = level_of(stream_key, extent, split, -0.22, 0.18) if split else 1.0
    values = jax.random.normal(stream_key, extent, jnp.float32) * scale * factor_of
    return jnp.minimum(jnp.maximum(values, -limit), limit).astype(kind)


def setup_inputs(seed: int = 0) -> dict:
    seeds = jax.random.split(jax.random.key(seed), 13)
    queries = draw_queries(jax.random.fold_in(seeds[12], 71), 0)
    resp_keys = draw_resp_keys(jax.random.fold_in(seeds[12], 71), 0)
    response_values = normal_values(seeds[2], (RESPONSE_COUNT, RESPONSE_LENGTH, KEY_VALUE_HEADS * HEAD_SIZE), 1.0, 6.0, ((0, 8), (1, 32)))
    prompt_keys = draw_prompt_keys(jax.random.fold_in(seeds[12], 71), 0)
    shared_prompt_values = normal_values(seeds[4], (PROMPT_LENGTH, KEY_VALUE_HEADS * HEAD_SIZE), 1.0, 6.0, ((0, 256),))
    value_head = normal_values(seeds[5], (QUERY_HEAD_COUNT * HEAD_SIZE,), (QUERY_HEAD_COUNT * HEAD_SIZE) ** -0.5, 0.09375, (), jnp.float32)
    token_ids = set_ends(skewed_wide(seeds[6], (RESPONSE_COUNT, RESPONSE_LENGTH), VOCAB, 2), jax.random.fold_in(seeds[6], 3), 0, VOCAB - 1).astype(jnp.int32)
    policy_logprobs = jnp.clip(-10.0 + 9.5 * jax.random.uniform(seeds[7], (RESPONSE_COUNT, RESPONSE_LENGTH), jnp.float32) ** level_of(seeds[7], (RESPONSE_COUNT, RESPONSE_LENGTH), ((0, 8), (1, 32)), -0.2, 0.2), -10.0, -0.5)
    ref_table = jnp.clip(jax.random.uniform(seeds[8], (VOCAB,), jnp.float32, -10.0, -0.5), -10.0, -0.5)
    scores = normal_values(seeds[9], (RESPONSE_COUNT,), 1.0, 4.0, ((0, 8),), jnp.float32)
    lengths = uneven_parts(seeds[10], RESPONSE_COUNT, (5 * RESPONSE_COUNT * RESPONSE_LENGTH) // 8, RESPONSE_LENGTH, 2).astype(jnp.int32)
    horizon = jnp.clip(jnp.exp(math.log(16384.0) - 6.015181 * jax.random.uniform(seeds[11], (RESPONSE_COUNT,), jnp.float32) ** level_of(seeds[11], (RESPONSE_COUNT,), ((0, 8),), -0.2, 0.2)), 40.0, 16384.0)
    return dict(queries=queries, resp_keys=resp_keys, response_values=response_values, prompt_keys=prompt_keys, shared_prompt_values=shared_prompt_values, value_head=value_head, token_ids=token_ids, policy_logprobs=policy_logprobs, ref_table=ref_table, scores=scores, lengths=lengths, horizon=horizon)


kl_beta = 0.01
masked_logit = -1e+30

def attend_rows(query_row_stack, key_row_stack, value_row_stack, allowed):
    row_number_total = query_row_stack.shape[0]
    query_group_width = QUERY_HEAD_COUNT // KEY_VALUE_HEADS
    query_partition = query_row_stack.astype(jnp.float32).reshape(row_number_total, KEY_VALUE_HEADS, query_group_width, HEAD_SIZE)
    key_per_head = key_row_stack.astype(jnp.float32).reshape(key_row_stack.shape[0], KEY_VALUE_HEADS, HEAD_SIZE)
    value_per_head = value_row_stack.astype(jnp.float32).reshape(value_row_stack.shape[0], KEY_VALUE_HEADS, HEAD_SIZE)
    attention_logits = jnp.einsum('ujpt,vjt->jpuv', query_partition, key_per_head) / math.sqrt(HEAD_SIZE)
    if allowed is not None:
        attention_logits = jnp.where(allowed, attention_logits, masked_logit)
    row_peak = lax.optimization_barrier(jnp.max(attention_logits, axis=-1))
    weights = jnp.exp(attention_logits - row_peak[..., None])
    denom_sum = lax.optimization_barrier(jnp.sum(weights, axis=-1))
    rounded_length = lax.optimization_barrier(weights.astype(jnp.bfloat16)).astype(jnp.float32)
    numerator_sum = jnp.einsum('tqps,stb->tqpb', rounded_length, value_per_head)
    normed = (numerator_sum / denom_sum[..., None]).transpose(2, 0, 1, 3).reshape(row_number_total, QUERY_HEAD_COUNT * HEAD_SIZE).astype(jnp.bfloat16)
    log_total = (row_peak + jnp.log(denom_sum)).transpose(2, 0, 1).reshape(row_number_total, QUERY_HEAD_COUNT)
    return (normed, log_total)

def merge_states(prompt_out, prompt_log, reply_out, reply_log):
    row_number_total = prompt_out.shape[0]
    top_log = jnp.maximum(prompt_log, reply_log)
    prompt_share = jnp.exp(prompt_log - top_log)
    reply_share = jnp.exp(reply_log - top_log)
    mixed = prompt_share[..., None] * prompt_out.astype(jnp.float32).reshape(row_number_total, QUERY_HEAD_COUNT, HEAD_SIZE)
    mixed = mixed + reply_share[..., None] * reply_out.astype(jnp.float32).reshape(row_number_total, QUERY_HEAD_COUNT, HEAD_SIZE)
    mixed = mixed / (prompt_share + reply_share)[..., None]
    return mixed.reshape(row_number_total, QUERY_HEAD_COUNT * HEAD_SIZE).astype(jnp.bfloat16)

def reference(queries, resp_keys, response_values, prompt_keys, shared_prompt_values, value_head, token_ids, policy_logprobs, ref_table, scores, lengths, horizon):
    block_size = math.gcd(RESPONSE_LENGTH, 256)
    positions = jnp.arange(RESPONSE_LENGTH, dtype=jnp.int32)

    def one_response(inputs):
        query_all, key_all, value_all, length = inputs

        def one_block(block_pair):
            query_row_stack, query_pos = block_pair
            prompt_out, prompt_log = attend_rows(query_row_stack, prompt_keys, shared_prompt_values, None)
            allowed = (positions[None, :] <= query_pos[:, None]) & (positions[None, :] < length)
            reply_out, reply_log = attend_rows(query_row_stack, key_all, value_all, allowed)
            return merge_states(prompt_out, prompt_log, reply_out, reply_log)
        mixed = lax.map(one_block, (query_all.reshape(RESPONSE_LENGTH // block_size, block_size, QUERY_HEAD_COUNT * HEAD_SIZE), positions.reshape(RESPONSE_LENGTH // block_size, block_size)))
        return mixed.reshape(RESPONSE_LENGTH, QUERY_HEAD_COUNT * HEAD_SIZE)
    attn_out = lax.map(one_response, (queries, resp_keys, response_values, lengths))
    is_live = positions[None, :] < lengths[:, None]
    raw_values = jnp.dot(attn_out.astype(jnp.float32).reshape(RESPONSE_COUNT * RESPONSE_LENGTH, QUERY_HEAD_COUNT * HEAD_SIZE), value_head, precision=lax.Precision.HIGHEST)
    values = jnp.where(is_live, raw_values.reshape(RESPONSE_COUNT, RESPONSE_LENGTH), 0.0)
    rewards = jnp.where(is_live, -kl_beta * (policy_logprobs - ref_table[token_ids]), 0.0)
    rewards = rewards + jnp.where(positions[None, :] == lengths[:, None] - 1, scores[:, None], 0.0)
    values_next = jnp.concatenate([values[:, 1:], jnp.zeros((RESPONSE_COUNT, 1), jnp.float32)], axis=1)
    deltas = jnp.where(is_live, rewards + values_next - values, 0.0)
    lam_step = jnp.exp(-1.0 / horizon)

    def scan_step(running_state, column):
        running_state = column + lam_step * running_state
        return (running_state, running_state)
    leftover, reversed_adv = lax.scan(scan_step, jnp.zeros((RESPONSE_COUNT,), jnp.float32), deltas.T, reverse=True)
    advantages = jnp.where(is_live, reversed_adv.T, 0.0)
    return (attn_out, values, advantages)
```

```python
import functools
import math

import jax
import jax.numpy as jnp
from jax import lax
from jax.experimental import pallas as pl
from jax.experimental.pallas import tpu as pltpu
from jax.sharding import PartitionSpec as P

F32 = jnp.float32
BF16 = jnp.bfloat16
MESH = pl.DeviceIdType.MESH

HEADS = 4
GROUP = 8
D = 128
NX, NY, NZ = 4, 4, 8
ROWS = 128
STACK = GROUP * ROWS
PROMPT = 2048
REPLY = 4096
SUPER = NZ * ROWS
CHUNK = 512
VOCAB = 128256
KL_BETA = 0.01
NEG = -1e30
SCALE = math.log2(math.e) / math.sqrt(D)


def fold(state, q, k, v, allowed):
    peak, total, acc = state
    s = lax.dot_general(q, k, (((1,), (1,)), ((), ())), preferred_element_type=F32)
    if allowed is not None:
        s = jnp.where(allowed, s, NEG)
    new = jnp.maximum(peak, jnp.max(s, axis=1, keepdims=True))
    w = jnp.exp2(s * SCALE - new * SCALE)
    shrink = jnp.exp2((peak - new) * SCALE)
    total = total * shrink + jnp.sum(w, axis=1, keepdims=True)
    acc = acc * shrink + jnp.dot(w.astype(BF16), v, preferred_element_type=F32)
    return new, total, acc


def stacked(qg, block):
    return jnp.concatenate([qg[block, :, j * D : (j + 1) * D] for j in range(GROUP)], axis=0)


def body(
    scores_ref, lengths_ref, horizon_ref, ids_smem, q_hbm, k_hbm, v_hbm, pk_ref, pv_ref, head_ref, ids_ref, logp_ref, table_hbm,
    attn_ref, values_ref, adv_ref,
    qg, kvg, pkv, pg, pk_all, pv_all, acc, peak, total, ob, og, table, picked, packet, packets,
    local_sem, qy_send, qy_recv, ky_send, ky_recv, py_send, py_recv, pz_send, pz_recv, px_send, px_recv,
    pc_send, pc_recv, ring_send, ring_recv, oy_send, oy_recv, gy_send, gy_recv, gz_send, gz_recv,
):
    r = lax.axis_index("resp")
    s = lax.axis_index("seq")
    x, c = r // 2, r % 2
    y, z = s // NZ, s % NZ
    ahead = lambda d: (r, lax.rem(y + d, NY) * NZ + z)
    along = lambda d: (r, y * NZ + lax.rem(z + d, NZ))
    across = lambda d: (lax.rem(x + d, NX) * 2 + c, s)
    twin = (x * 2 + (1 - c), s)

    def remote(src, dst, send, recv, device):
        copy = pltpu.make_async_remote_copy(
            src_ref=src, dst_ref=dst, send_sem=send, recv_sem=recv, device_id=device, device_id_type=MESH
        )
        copy.start()
        return copy

    def head_cols(h, width):
        return pl.ds(pl.multiple_of(h * width, width), width)

    own = [
        pltpu.make_async_copy(q_hbm.at[0, :, head_cols(y, STACK)], qg.at[y], local_sem.at[0]),
        pltpu.make_async_copy(k_hbm.at[0, :, head_cols(y, D)], kvg.at[0, y, z], local_sem.at[1]),
        pltpu.make_async_copy(v_hbm.at[0, :, head_cols(y, D)], kvg.at[1, y, z], local_sem.at[2]),
        pltpu.make_async_copy(table_hbm, table, local_sem.at[3]),
    ]
    for copy in own:
        copy.start()
    for h in range(HEADS):
        cols = slice(h * D, (h + 1) * D)
        pkv[h] = jnp.concatenate([pk_ref[:, cols].astype(F32), pv_ref[:, cols].astype(F32)], axis=0).astype(BF16)
    pg[x, c, z, y] = pkv[y]

    barrier = pltpu.get_barrier_semaphore()
    peers = [ahead(d) for d in range(1, NY)] + [along(d) for d in range(1, NZ)] + [across(d) for d in range(1, NX)] + [twin]
    for peer in peers:
        pl.semaphore_signal(barrier, inc=1, device_id=peer, device_id_type=MESH)
    pl.semaphore_wait(barrier, len(peers))

    sent = []
    p_y, k_y, q_y = [], [], []
    for d in range(1, NY):
        to = lax.rem(y + d, NY)
        p_y.append(remote(pkv.at[to], pg.at[x, c, z, y], py_send.at[d - 1], py_recv.at[d - 1], ahead(d)))
    for d in range(1, NY):
        to = lax.rem(y + d, NY)
        for i, src in enumerate((k_hbm, v_hbm)):
            k_y.append(
                remote(
                    src.at[0, :, head_cols(to, D)], kvg.at[i, y, z],
                    ky_send.at[d - 1, i], ky_recv.at[d - 1, i], ahead(d),
                )
            )
    for d in (1, 3, 2):
        to = lax.rem(y + d, NY)
        q_y.append(remote(q_hbm.at[0, :, head_cols(to, STACK)], qg.at[y], qy_send.at[d - 1], qy_recv.at[d - 1], ahead(d)))
    sent += p_y + k_y + q_y

    for copy in p_y:
        copy.wait_recv()
    p_z = [remote(pg.at[x, c, z], pg.at[x, c, z], pz_send.at[d - 1], pz_recv.at[d - 1], along(d)) for d in range(1, NZ)]
    sent += p_z
    for copy in own[1:3]:
        copy.wait()
    for copy in k_y:
        copy.wait_recv()

    def ring_step(step):
        back = lax.rem(z - step + NZ, NZ)
        fore = lax.rem(z + step, NZ)
        if step < NZ // 2 - 1:
            parts = (kvg.at[:, :, back], kvg.at[:, :, fore])
        else:
            parts = (kvg.at[0, :, back], kvg.at[1, :, fore])
        out = [
            remote(parts[0], parts[0], ring_send.at[step, 0], ring_recv.at[step, 0], along(1)),
            remote(parts[1], parts[1], ring_send.at[step, 1], ring_recv.at[step, 1], along(NZ - 1)),
        ]
        sent.extend(out)
        return out

    ring = ring_step(0)
    for copy in p_z:
        copy.wait_recv()
    p_x = [remote(pg.at[x, c], pg.at[x, c], px_send.at[d - 1], px_recv.at[d - 1], across(d)) for d in (1, 3, 2)]
    p_c = [remote(pg.at[x, c], pg.at[x, c], pc_send.at[0], pc_recv.at[0], twin)]

    own[3].wait()

    def pick(t, carry):
        row = ids_smem[0, t] // D
        picked[pl.ds(t, 1), :] = table[pl.ds(row, 1), :]
        return carry

    lax.fori_loop(0, ROWS, pick, 0)

    for i, d in enumerate((1, 3, 2)):
        p_x[i].wait_recv()
        src = lax.rem(x - d + NX, NX)
        p_c.append(remote(pg.at[src, c], pg.at[src, c], pc_send.at[d], pc_recv.at[d], twin))
    sent += p_x + p_c
    for copy in p_c:
        copy.wait_recv()
    for part in range(NX):
        both = pg[part].astype(F32).reshape(2 * NZ * NY, 16, D)
        rows = slice(part * 512, (part + 1) * 512)
        pk_all[rows, :] = both[:, :8, :].reshape(512, D).astype(BF16)
        pv_all[rows, :] = both[:, 8:, :].reshape(512, D).astype(BF16)

    def prompt_pass(block):
        q = stacked(qg, block)
        state = (jnp.full((STACK, 1), NEG, F32), jnp.zeros((STACK, 1), F32), jnp.zeros((STACK, D), F32))
        for i in range(PROMPT // CHUNK):
            rows = slice(i * CHUNK, (i + 1) * CHUNK)
            state = fold(state, q, pk_all[rows, :], pv_all[rows, :], None)
        peak[block], total[block], acc[block] = state

    for step, d in enumerate((0, 3, 1, 2)):
        if step == 0:
            own[0].wait()
        else:
            q_y[{1: 0, 3: 1, 2: 2}[d]].wait_recv()
        prompt_pass(lax.rem(y - d + NY, NY))
        for copy in ring:
            copy.wait_recv()
        if step < NZ // 2 - 1:
            ring = ring_step(step + 1)

    length = lengths_ref[0]
    lanes = lax.broadcasted_iota(jnp.int32, (1, CHUNK), 1)
    tri = lax.broadcasted_iota(jnp.int32, (ROWS, CHUNK), 1) - lax.broadcasted_iota(jnp.int32, (ROWS, CHUNK), 0)
    per_super = SUPER // CHUNK
    per_chunk = CHUNK // ROWS

    def reply_pass(block):
        q = stacked(qg, block)

        def kv(sup, i):
            zs = slice(i * per_chunk, (i + 1) * per_chunk)
            return kvg[0, sup, zs].reshape(CHUNK, D), kvg[1, sup, zs].reshape(CHUNK, D)

        def whole(sup, state):
            for i in range(per_super):
                k, v = kv(sup, i)
                state = fold(state, q, k, v, sup * SUPER + i * CHUNK + lanes < length)
            return state

        state = lax.fori_loop(0, block, whole, (peak[block], total[block], acc[block]))
        for i in range(per_super):
            k, v = kv(block, i)
            allowed = (tri <= z * ROWS - i * CHUNK) & (block * SUPER + i * CHUNK + lanes < length)
            state = fold(state, q, k, v, jnp.concatenate([allowed] * GROUP, axis=0))
        out = (state[2] / state[1]).astype(BF16)
        return [out[j * ROWS : (j + 1) * ROWS] for j in range(GROUP)]

    o_y = []
    for d in (2, 1, 3):
        to = lax.rem(y + d, NY)
        for j, part in enumerate(reply_pass(to)):
            ob[d - 1, :, j * D : (j + 1) * D] = part
        o_y.append(remote(ob.at[d - 1], og.at[y], oy_send.at[d - 1], oy_recv.at[d - 1], ahead(d)))
    for j, part in enumerate(reply_pass(y)):
        og[y, :, j * D : (j + 1) * D] = part
    sent += o_y
    for copy in o_y:
        copy.wait_recv()
    back_home = [
        pltpu.make_async_copy(og.at[h], attn_ref.at[0, :, h * STACK : (h + 1) * STACK], local_sem.at[4 + h])
        for h in range(HEADS)
    ]
    for copy in back_home:
        copy.start()

    value = jnp.zeros((ROWS, 1), F32)
    for h in range(HEADS):
        value = value + jnp.sum(og[h].astype(F32) * head_ref[:, h * STACK : (h + 1) * STACK], axis=1, keepdims=True)
    sub = lax.broadcasted_iota(jnp.int32, (ROWS, ROWS), 0)
    lane = lax.broadcasted_iota(jnp.int32, (ROWS, ROWS), 1)
    as_row = lambda column, shift=0: jnp.sum(jnp.where(sub == lane + shift, column, 0.0), axis=0, keepdims=True)
    as_column = lambda row: jnp.sum(jnp.where(sub == lane, row, 0), axis=1, keepdims=True)
    place = s * ROWS + lax.broadcasted_iota(jnp.int32, (1, ROWS), 1)
    live = place < length
    value = jnp.where(s * ROWS + lax.broadcasted_iota(jnp.int32, (ROWS, 1), 0) < length, value, 0.0)
    value_row = as_row(value)
    values_ref[...] = value_row
    spot = as_column(ids_ref[...] % D)
    reference = as_row(jnp.sum(jnp.where(lane == spot, picked[...], 0.0), axis=1, keepdims=True))
    rewards = jnp.where(live, -KL_BETA * (logp_ref[...] - reference), 0.0)
    rewards = rewards + jnp.where(place == length - 1, scores_ref[0], 0.0)
    deltas = jnp.where(live, rewards + as_row(value, 1) - value_row, 0.0)
    rate = -1.0 / jnp.full((1, 1), horizon_ref[0], F32)
    gap = (lane - sub).astype(F32)
    decay = jnp.where(gap >= 0.0, jnp.exp(jnp.maximum(gap, 0.0) * rate), 0.0)
    local_adv = as_row(jnp.sum(decay * deltas, axis=1, keepdims=True))
    first = lax.broadcasted_iota(jnp.int32, (8, ROWS), 1)
    packet[...] = jnp.where(first == 0, local_adv[:, :1], jnp.where(first == 1, value_row[:, :1], 0.0))
    packets[z, y] = packet[...]

    g_y = [remote(packet, packets.at[z, y], gy_send.at[d - 1], gy_recv.at[d - 1], ahead(d)) for d in range(1, NY)]
    for copy in g_y:
        copy.wait_recv()
    g_z = [remote(packets.at[z], packets.at[z], gz_send.at[d - 1], gz_recv.at[d - 1], along(d)) for d in range(1, NZ)]
    for copy in g_z:
        copy.wait_recv()
    sent += g_y + g_z

    carry = jnp.zeros((1, 1), F32)
    beyond = jnp.zeros((1, 1), F32)
    for yy in range(NY):
        rows = packets[:, yy, 0, :]
        far = (yy * NZ + lax.broadcasted_iota(jnp.int32, (NZ, 1), 0) - s - 1).astype(F32)
        adv_weight = jnp.where(far >= 0.0, jnp.exp(jnp.maximum(far, 0.0) * ROWS * rate), 0.0)
        value_weight = jnp.where(far >= 1.0, jnp.exp((jnp.maximum(far - 1.0, 0.0) * ROWS + (ROWS - 1)) * rate), 0.0)
        carry = carry + jnp.sum(adv_weight * rows[:, :1] + value_weight * rows[:, 1:2], axis=0, keepdims=True)
        beyond = beyond + jnp.sum(jnp.where(far == 0.0, rows[:, 1:2], 0.0), axis=0, keepdims=True)
    along_row = lax.broadcasted_iota(jnp.int32, (1, ROWS), 1).astype(F32)
    tail = jnp.exp((ROWS - 1 - along_row) * rate) * beyond + jnp.exp((ROWS - along_row) * rate) * carry
    adv_ref[...] = jnp.where(live, local_adv + tail, 0.0)

    for copy in back_home:
        copy.wait()
    for copy in sent:
        copy.wait_send()


def local(queries, resp_keys, response_values, prompt_keys, prompt_values, value_head, token_ids, logprobs, ref_table, scores, lengths, horizon):
    smem = pl.BlockSpec(memory_space=pltpu.SMEM)
    vmem = pl.BlockSpec(memory_space=pltpu.VMEM)
    hbm = pl.BlockSpec(memory_space=pl.ANY)
    dma = pltpu.SemaphoreType.DMA
    return pl.pallas_call(
        body,
        out_shape=(
            jax.ShapeDtypeStruct((1, ROWS, HEADS * STACK), BF16),
            jax.ShapeDtypeStruct((1, ROWS), F32),
            jax.ShapeDtypeStruct((1, ROWS), F32),
        ),
        in_specs=[smem, smem, smem, smem, hbm, hbm, hbm, vmem, vmem, vmem, vmem, vmem, hbm],
        out_specs=(hbm, vmem, vmem),
        scratch_shapes=[
            pltpu.VMEM((NY, ROWS, STACK), BF16),
            pltpu.VMEM((2, NY, NZ, ROWS, D), BF16),
            pltpu.VMEM((HEADS, 16, D), BF16),
            pltpu.VMEM((NX, 2, NZ, NY, 16, D), BF16),
            pltpu.VMEM((PROMPT, D), BF16),
            pltpu.VMEM((PROMPT, D), BF16),
            pltpu.VMEM((NY, STACK, D), F32),
            pltpu.VMEM((NY, STACK, 1), F32),
            pltpu.VMEM((NY, STACK, 1), F32),
            pltpu.VMEM((NY - 1, ROWS, STACK), BF16),
            pltpu.VMEM((HEADS, ROWS, STACK), BF16),
            pltpu.VMEM((VOCAB // D, D), F32),
            pltpu.VMEM((ROWS, D), F32),
            pltpu.VMEM((8, ROWS), F32),
            pltpu.VMEM((NZ, NY, 8, ROWS), F32),
            dma((8,)),
            dma((NY - 1,)), dma((NY - 1,)),
            dma((NY - 1, 2)), dma((NY - 1, 2)),
            dma((NY - 1,)), dma((NY - 1,)),
            dma((NZ - 1,)), dma((NZ - 1,)),
            dma((NX - 1,)), dma((NX - 1,)),
            dma((NX,)), dma((NX,)),
            dma((NZ // 2, 2)), dma((NZ // 2, 2)),
            dma((NY - 1,)), dma((NY - 1,)),
            dma((NY - 1,)), dma((NY - 1,)),
            dma((NZ - 1,)), dma((NZ - 1,)),
        ],
        compiler_params=pltpu.CompilerParams(
            collective_id=0, has_side_effects=True, vmem_limit_bytes=56 * 2**20
        ),
    )(
        scores, lengths, horizon, token_ids, queries, resp_keys, response_values, prompt_keys, prompt_values,
        value_head.reshape(1, HEADS * STACK), token_ids, logprobs, ref_table.reshape(VOCAB // D, D),
    )


def solution(mesh):
    return jax.shard_map(
        local,
        mesh=mesh,
        in_specs=(
            P("resp", "seq", None),
            P("resp", "seq", None),
            P("resp", "seq", None),
            P(("resp", "seq"), None),
            P(("resp", "seq"), None),
            P(),
            P("resp", "seq"),
            P("resp", "seq"),
            P(),
            P("resp"),
            P("resp"),
            P("resp"),
        ),
        out_specs=(P("resp", "seq", None), P("resp", "seq"), P("resp", "seq")),
        check_vma=False,
    )
```

```python
import functools
import math

import jax
import jax.numpy as jnp
from jax import lax
from jax.experimental import pallas as pl
from jax.experimental.pallas import tpu as pltpu
from jax.sharding import PartitionSpec as P

F32 = jnp.float32
BF16 = jnp.bfloat16
MESH = pl.DeviceIdType.MESH

HEADS = 4
GROUP = 8
D = 128
NX, NY, NZ = 4, 4, 8
ROWS = 128
STACK = GROUP * ROWS
PROMPT = 2048
REPLY = 4096
SUPER = NZ * ROWS
HALF = NZ // 2
CHUNK = 512
VOCAB = 128256
KL_BETA = 0.01
NEG = -1e30
SCALE = math.log2(math.e) / math.sqrt(D)


def fold(state, q, k, v, bias=None):
    peak, total, acc = state
    s = lax.dot_general(q, k, (((1,), (1,)), ((), ())), preferred_element_type=F32)
    if bias is not None:
        s = (s.reshape(GROUP, ROWS, CHUNK) + bias[None]).reshape(STACK, CHUNK)
    new = jnp.maximum(peak, jnp.max(s, axis=1, keepdims=True))
    scaled = new * SCALE
    w = jnp.exp2(s * SCALE - jnp.concatenate([scaled] * (CHUNK // D), axis=1))
    shrink = jnp.exp2(peak * SCALE - scaled)
    total = total * shrink + jnp.sum(w, axis=1, keepdims=True)
    acc = acc * shrink + jnp.dot(w.astype(BF16), v, preferred_element_type=F32)
    return new, total, acc


def stacked(qg, block):
    return jnp.concatenate([qg[block, :, j * D : (j + 1) * D] for j in range(GROUP)], axis=0)


def body(
    scores_ref, lengths_ref, horizon_ref, ids_smem, q_hbm, k_hbm, v_hbm, pk_ref, pv_ref, head_ref, ids_ref, logp_ref, table_hbm,
    attn_ref, values_ref, adv_ref,
    qg, kvg, pkv, pg, pk_all, pv_all, acc, peak, total, staged, past, causal, ob, og, table, picked, packet, packets,
    local_sem, qy_send, qy_recv, ky_send, ky_recv, py_send, py_recv, pz_send, pz_recv, px_send, px_recv,
    pc_send, pc_recv, ring_send, ring_recv, oy_send, oy_recv, gy_send, gy_recv, gz_send, gz_recv,
):
    r = lax.axis_index("resp")
    s = lax.axis_index("seq")
    x, c = r // 2, r % 2
    y, z = s // NZ, s % NZ
    ahead = lambda d: (r, lax.rem(y + d, NY) * NZ + z)
    along = lambda d: (r, y * NZ + lax.rem(z + d, NZ))
    across = lambda d: (lax.rem(x + d, NX) * 2 + c, s)
    twin = (x * 2 + (1 - c), s)

    def remote(src, dst, send, recv, device):
        copy = pltpu.make_async_remote_copy(
            src_ref=src, dst_ref=dst, send_sem=send, recv_sem=recv, device_id=device, device_id_type=MESH
        )
        copy.start()
        return copy

    def head_cols(h, width):
        return pl.ds(pl.multiple_of(h * width, width), width)

    own = [
        pltpu.make_async_copy(q_hbm.at[0, :, head_cols(y, STACK)], qg.at[y], local_sem.at[0]),
        pltpu.make_async_copy(k_hbm.at[0, :, head_cols(y, D)], kvg.at[0, y, z], local_sem.at[1]),
        pltpu.make_async_copy(v_hbm.at[0, :, head_cols(y, D)], kvg.at[1, y, z], local_sem.at[2]),
        pltpu.make_async_copy(table_hbm, table, local_sem.at[3]),
    ]
    for copy in own:
        copy.start()
    barrier = pltpu.get_barrier_semaphore()
    peers = [ahead(d) for d in range(1, NY)] + [along(d) for d in range(1, NZ)] + [across(d) for d in range(1, NX)] + [twin]
    for peer in peers:
        pl.semaphore_signal(barrier, inc=1, device_id=peer, device_id_type=MESH)

    for h in range(HEADS):
        cols = slice(h * D, (h + 1) * D)
        pkv[h] = jnp.concatenate([pk_ref[:, cols].astype(F32), pv_ref[:, cols].astype(F32)], axis=0).astype(BF16)
    pg[x, c, z, y] = pkv[y]

    order = [lax.rem(z + k + NZ, NZ) for k in (0, 1, -1, 2, -2, 3, -3, 4)]
    inside = lax.broadcasted_iota(jnp.int32, (ROWS, ROWS), 1) - lax.broadcasted_iota(jnp.int32, (ROWS, ROWS), 0)
    for k in range(NZ):
        causal[k // HALF, :, (k % HALF) * ROWS : (k % HALF + 1) * ROWS] = jnp.where(inside <= (z - order[k]) * ROWS, 0.0, NEG)

    own[3].wait()

    def pick(t, carry):
        row = ids_smem[0, t] // D
        picked[pl.ds(t, 1), :] = table[pl.ds(row, 1), :]
        return carry

    lax.fori_loop(0, ROWS, pick, 0)
    pl.semaphore_wait(barrier, len(peers))

    sent = []
    p_y, k_y, q_y = [], [], {}
    for d in range(1, NY):
        to = lax.rem(y + d, NY)
        p_y.append(remote(pkv.at[to], pg.at[x, c, z, y], py_send.at[d - 1], py_recv.at[d - 1], ahead(d)))
    for d in range(1, NY):
        to = lax.rem(y + d, NY)
        for i, src in enumerate((k_hbm, v_hbm)):
            k_y.append(
                remote(
                    src.at[0, :, head_cols(to, D)], kvg.at[i, y, z],
                    ky_send.at[d - 1, i], ky_recv.at[d - 1, i], ahead(d),
                )
            )
    for d in (1, 3, 2):
        to = lax.rem(y + d, NY)
        q_y[d] = remote(q_hbm.at[0, :, head_cols(to, STACK)], qg.at[y], qy_send.at[d - 1], qy_recv.at[d - 1], ahead(d))
    sent += p_y + k_y + list(q_y.values())

    for copy in p_y:
        copy.wait_recv()
    p_z = [remote(pg.at[x, c, z], pg.at[x, c, z], pz_send.at[d - 1], pz_recv.at[d - 1], along(d)) for d in range(1, NZ)]
    sent += p_z
    for copy in own[1:3]:
        copy.wait()
    for copy in k_y:
        copy.wait_recv()

    def ring_step(step):
        back = lax.rem(z - step + NZ, NZ)
        fore = lax.rem(z + step, NZ)
        if step < NZ // 2 - 1:
            parts = (kvg.at[:, :, back], kvg.at[:, :, fore])
        else:
            parts = (kvg.at[0, :, back], kvg.at[1, :, fore])
        out = [
            remote(parts[0], parts[0], ring_send.at[step, 0], ring_recv.at[step, 0], along(1)),
            remote(parts[1], parts[1], ring_send.at[step, 1], ring_recv.at[step, 1], along(NZ - 1)),
        ]
        sent.extend(out)
        return out

    ring = ring_step(0)
    for copy in p_z:
        copy.wait_recv()
    p_x = {d: remote(pg.at[x, c], pg.at[x, c], px_send.at[d - 1], px_recv.at[d - 1], across(d)) for d in (1, 3, 2)}
    p_c = {0: remote(pg.at[x, c], pg.at[x, c], pc_send.at[0], pc_recv.at[0], twin)}

    def pass_over(d):
        p_x[d].wait_recv()
        src = lax.rem(x - d + NX, NX)
        p_c[d] = remote(pg.at[src, c], pg.at[src, c], pc_send.at[d], pc_recv.at[d], twin)

    def unpack(i, d):
        p_c[d].wait_recv()
        both = pg[lax.rem(x - d + NX, NX)].astype(F32).reshape(2 * NZ * NY, 16, D)
        pk_all[i] = both[:, :8, :].reshape(CHUNK, D).astype(BF16)
        pv_all[i] = both[:, 8:, :].reshape(CHUNK, D).astype(BF16)

    def prompt_fold(i, d):
        block = lax.rem(y - d + NY, NY)
        if i == 0:
            if d == 0:
                own[0].wait()
            else:
                q_y[d].wait_recv()
            state = (jnp.full((STACK, D), NEG, F32), jnp.zeros((STACK, D), F32), jnp.zeros((STACK, D), F32))
        else:
            state = (peak[block], total[block], acc[block])
        peak[block], total[block], acc[block] = fold(state, stacked(qg, block), pk_all[i], pv_all[i])

    def ring_on(step):
        for copy in ring:
            copy.wait_recv()
        return ring_step(step)

    unpack(0, 0)
    prompt_fold(0, 0)
    pass_over(1)
    prompt_fold(0, 1)
    pass_over(3)
    prompt_fold(0, 3)
    ring = ring_on(1)
    pass_over(2)
    unpack(1, 1)
    for d in (0, 1, 3):
        prompt_fold(1, d)
    unpack(2, 3)
    prompt_fold(2, 0)
    ring = ring_on(2)
    for d in (1, 3):
        prompt_fold(2, d)
    for i in range(3):
        prompt_fold(i, 2)
    ring = ring_on(3)
    unpack(3, 2)
    for d in (0, 1, 3, 2):
        prompt_fold(3, d)
    sent += list(p_x.values()) + list(p_c.values())

    length = lengths_ref[0]
    lanes = lax.broadcasted_iota(jnp.int32, (1, ROWS), 1)

    def turn(t):
        return lax.rem(2 + 3 * t + 3 * (t * (t - 1) // 2), NY)

    def reply_half(half):
        for sup in range(NY):
            for k in range(HALF):
                rows = slice(k * ROWS, (k + 1) * ROWS)
                zz = order[half * HALF + k]
                staged[0, sup, rows] = kvg[0, sup, zz]
                staged[1, sup, rows] = kvg[1, sup, zz]
                past[sup, :, rows] = jnp.where(sup * SUPER + zz * ROWS + lanes < length, 0.0, NEG)

        def run(block):
            q = stacked(qg, block)
            state = (peak[block], total[block], acc[block])
            for sup in range(block):
                state = fold(state, q, staged[0, sup], staged[1, sup], past[sup])
            state = fold(state, q, staged[0, block], staged[1, block], causal[half] + past[block])
            peak[block], total[block], acc[block] = state

        def step(t, carry):
            d = turn(t)
            block = lax.rem(y + d, NY)
            lax.switch(block, [functools.partial(run, b) for b in range(NY)])
            if half == 1:
                out = (acc[block] / total[block]).astype(BF16)
                for j in range(GROUP):
                    ob[t, :, j * D : (j + 1) * D] = out[j * ROWS : (j + 1) * ROWS]

                @pl.when(t < NY - 1)
                def _():
                    home(t).start()

            return carry

        lax.fori_loop(0, NY, step, 0)

    def home(t):
        return pltpu.make_async_remote_copy(
            src_ref=ob.at[t], dst_ref=og.at[y], send_sem=oy_send.at[t], recv_sem=oy_recv.at[t],
            device_id=ahead(turn(t)), device_id_type=MESH,
        )

    reply_half(0)
    for copy in ring:
        copy.wait_recv()
    reply_half(1)
    og[y] = ob[NY - 1]
    o_y = [home(t) for t in range(NY - 1)]
    sent += o_y
    for copy in o_y:
        copy.wait_recv()
    back_home = [
        pltpu.make_async_copy(og.at[h], attn_ref.at[0, :, h * STACK : (h + 1) * STACK], local_sem.at[4 + h])
        for h in range(HEADS)
    ]
    for copy in back_home:
        copy.start()

    value = jnp.zeros((ROWS, 1), F32)
    for h in range(HEADS):
        value = value + jnp.sum(og[h].astype(F32) * head_ref[:, h * STACK : (h + 1) * STACK], axis=1, keepdims=True)
    sub = lax.broadcasted_iota(jnp.int32, (ROWS, ROWS), 0)
    lane = lax.broadcasted_iota(jnp.int32, (ROWS, ROWS), 1)
    as_row = lambda column, shift=0: jnp.sum(jnp.where(sub == lane + shift, column, 0.0), axis=0, keepdims=True)
    as_column = lambda row: jnp.sum(jnp.where(sub == lane, row, 0), axis=1, keepdims=True)
    place = s * ROWS + lax.broadcasted_iota(jnp.int32, (1, ROWS), 1)
    live = place < length
    value = jnp.where(s * ROWS + lax.broadcasted_iota(jnp.int32, (ROWS, 1), 0) < length, value, 0.0)
    value_row = as_row(value)
    values_ref[...] = value_row
    spot = as_column(ids_ref[...] % D)
    reference = as_row(jnp.sum(jnp.where(lane == spot, picked[...], 0.0), axis=1, keepdims=True))
    rewards = jnp.where(live, -KL_BETA * (logp_ref[...] - reference), 0.0)
    rewards = rewards + jnp.where(place == length - 1, scores_ref[0], 0.0)
    deltas = jnp.where(live, rewards + as_row(value, 1) - value_row, 0.0)
    rate = -1.0 / jnp.full((1, 1), horizon_ref[0], F32)
    gap = (lane - sub).astype(F32)
    decay = jnp.where(gap >= 0.0, jnp.exp(jnp.maximum(gap, 0.0) * rate), 0.0)
    local_adv = as_row(jnp.sum(decay * deltas, axis=1, keepdims=True))
    first = lax.broadcasted_iota(jnp.int32, (8, ROWS), 1)
    packet[...] = jnp.where(first == 0, local_adv[:, :1], jnp.where(first == 1, value_row[:, :1], 0.0))
    packets[z, y] = packet[...]

    g_y = [remote(packet, packets.at[z, y], gy_send.at[d - 1], gy_recv.at[d - 1], ahead(d)) for d in range(1, NY)]
    for copy in g_y:
        copy.wait_recv()
    g_z = [remote(packets.at[z], packets.at[z], gz_send.at[d - 1], gz_recv.at[d - 1], along(d)) for d in range(1, NZ)]
    for copy in g_z:
        copy.wait_recv()
    sent += g_y + g_z

    carry = jnp.zeros((1, 1), F32)
    beyond = jnp.zeros((1, 1), F32)
    for yy in range(NY):
        rows = packets[:, yy, 0, :]
        far = (yy * NZ + lax.broadcasted_iota(jnp.int32, (NZ, 1), 0) - s - 1).astype(F32)
        adv_weight = jnp.where(far >= 0.0, jnp.exp(jnp.maximum(far, 0.0) * ROWS * rate), 0.0)
        value_weight = jnp.where(far >= 1.0, jnp.exp((jnp.maximum(far - 1.0, 0.0) * ROWS + (ROWS - 1)) * rate), 0.0)
        carry = carry + jnp.sum(adv_weight * rows[:, :1] + value_weight * rows[:, 1:2], axis=0, keepdims=True)
        beyond = beyond + jnp.sum(jnp.where(far == 0.0, rows[:, 1:2], 0.0), axis=0, keepdims=True)
    along_row = lax.broadcasted_iota(jnp.int32, (1, ROWS), 1).astype(F32)
    tail = jnp.exp((ROWS - 1 - along_row) * rate) * beyond + jnp.exp((ROWS - along_row) * rate) * carry
    adv_ref[...] = jnp.where(live, local_adv + tail, 0.0)

    for copy in back_home:
        copy.wait()
    for copy in sent:
        copy.wait_send()


def local(queries, resp_keys, response_values, prompt_keys, prompt_values, value_head, token_ids, logprobs, ref_table, scores, lengths, horizon):
    smem = pl.BlockSpec(memory_space=pltpu.SMEM)
    vmem = pl.BlockSpec(memory_space=pltpu.VMEM)
    hbm = pl.BlockSpec(memory_space=pl.ANY)
    dma = pltpu.SemaphoreType.DMA
    return pl.pallas_call(
        body,
        out_shape=(
            jax.ShapeDtypeStruct((1, ROWS, HEADS * STACK), BF16),
            jax.ShapeDtypeStruct((1, ROWS), F32),
            jax.ShapeDtypeStruct((1, ROWS), F32),
        ),
        in_specs=[smem, smem, smem, smem, hbm, hbm, hbm, vmem, vmem, vmem, vmem, vmem, hbm],
        out_specs=(hbm, vmem, vmem),
        scratch_shapes=[
            pltpu.VMEM((NY, ROWS, STACK), BF16),
            pltpu.VMEM((2, NY, NZ, ROWS, D), BF16),
            pltpu.VMEM((HEADS, 16, D), BF16),
            pltpu.VMEM((NX, 2, NZ, NY, 16, D), BF16),
            pltpu.VMEM((PROMPT // CHUNK, CHUNK, D), BF16),
            pltpu.VMEM((PROMPT // CHUNK, CHUNK, D), BF16),
            pltpu.VMEM((NY, STACK, D), F32),
            pltpu.VMEM((NY, STACK, D), F32),
            pltpu.VMEM((NY, STACK, D), F32),
            pltpu.VMEM((2, NY, CHUNK, D), BF16),
            pltpu.VMEM((NY, 1, CHUNK), F32),
            pltpu.VMEM((2, ROWS, CHUNK), F32),
            pltpu.VMEM((NY, ROWS, STACK), BF16),
            pltpu.VMEM((HEADS, ROWS, STACK), BF16),
            pltpu.VMEM((VOCAB // D, D), F32),
            pltpu.VMEM((ROWS, D), F32),
            pltpu.VMEM((8, ROWS), F32),
            pltpu.VMEM((NZ, NY, 8, ROWS), F32),
            dma((8,)),
            dma((NY - 1,)), dma((NY - 1,)),
            dma((NY - 1, 2)), dma((NY - 1, 2)),
            dma((NY - 1,)), dma((NY - 1,)),
            dma((NZ - 1,)), dma((NZ - 1,)),
            dma((NX - 1,)), dma((NX - 1,)),
            dma((NX,)), dma((NX,)),
            dma((NZ // 2, 2)), dma((NZ // 2, 2)),
            dma((NY - 1,)), dma((NY - 1,)),
            dma((NY - 1,)), dma((NY - 1,)),
            dma((NZ - 1,)), dma((NZ - 1,)),
        ],
        compiler_params=pltpu.CompilerParams(
            collective_id=0, has_side_effects=True, vmem_limit_bytes=56 * 2**20
        ),
    )(
        scores, lengths, horizon, token_ids, queries, resp_keys, response_values, prompt_keys, prompt_values,
        value_head.reshape(1, HEADS * STACK), token_ids, logprobs, ref_table.reshape(VOCAB // D, D),
    )


def solution(mesh):
    return jax.shard_map(
        local,
        mesh=mesh,
        in_specs=(
            P("resp", "seq", None),
            P("resp", "seq", None),
            P("resp", "seq", None),
            P(("resp", "seq"), None),
            P(("resp", "seq"), None),
            P(),
            P("resp", "seq"),
            P("resp", "seq"),
            P(),
            P("resp"),
            P("resp"),
            P("resp"),
        ),
        out_specs=(P("resp", "seq", None), P("resp", "seq"), P("resp", "seq")),
        check_vma=False,
    )
```

```python
import functools
import math

import jax
import jax.numpy as jnp
from jax import lax
from jax.experimental import pallas as pl
from jax.experimental.pallas import tpu as pltpu
from jax.sharding import PartitionSpec as P

F32 = jnp.float32
BF16 = jnp.bfloat16
MESH = pl.DeviceIdType.MESH

HEADS = 4
GROUP = 8
D = 128
NX, NY, NZ = 4, 4, 8
SEQ = NY * NZ
ROWS = 128
STACK = GROUP * ROWS
PROMPT = 2048
REPLY = 4096
SUPER = NZ * ROWS
HALF = NZ // 2
CHUNK = 512
SHARE = 256
WING = STACK // 2
VOCAB = 128256
KL_BETA = 0.01
NEG = -1e30
SCALE = math.log2(math.e) / math.sqrt(D)


def fold(state, q, k, v, bias=None):
    peak, total, acc = state
    s = lax.dot_general(q, k, (((1,), (1,)), ((), ())), preferred_element_type=F32)
    if bias is not None:
        s = (s.reshape(GROUP, ROWS, -1) + bias[None]).reshape(s.shape)
    new = jnp.maximum(peak, jnp.max(s, axis=1, keepdims=True))
    scaled = new * SCALE
    w = jnp.exp2(s * SCALE - jnp.concatenate([scaled] * (s.shape[1] // D), axis=1))
    shrink = jnp.exp2(peak * SCALE - scaled)
    total = total * shrink + jnp.sum(w, axis=1, keepdims=True)
    acc = acc * shrink + jnp.dot(w.astype(BF16), v, preferred_element_type=F32)
    return new, total, acc


def stacked(qg, block):
    return jnp.concatenate([qg[block, :, j * D : (j + 1) * D] for j in range(GROUP)], axis=0)


def body(
    scores_ref, lengths_ref, horizon_ref, ids_smem, q_hbm, k_hbm, v_hbm, pk_ref, pv_ref, head_ref, ids_ref, logp_ref, table_hbm,
    attn_ref, values_ref, adv_ref,
    qg, kvg, pkv, pg, pk_all, pv_all, acc, peak, total, staged, past, causal, ob, og, table, picked, packet, packets,
    relay, local_sem, qy_send, qy_recv, ky_send, ky_recv, p_send, p_recv, px_send, px_recv,
    pc_send, pc_recv, ring_send, ring_recv, oy_send, oy_recv, g_send, g_recv,
):
    r = lax.axis_index("resp")
    s = lax.axis_index("seq")
    x, c = r // 2, r % 2
    y, z = s // NZ, s % NZ
    ahead = lambda d: (r, lax.rem(y + d, NY) * NZ + z)
    along = lambda d: (r, y * NZ + lax.rem(z + d, NZ))
    across = lambda d: (lax.rem(x + d, NX) * 2 + c, s)
    twin = (x * 2 + (1 - c), s)

    def remote(src, dst, send, recv, device):
        copy = pltpu.make_async_remote_copy(
            src_ref=src, dst_ref=dst, send_sem=send, recv_sem=recv, device_id=device, device_id_type=MESH
        )
        copy.start()
        return copy

    def head_cols(h, width):
        return pl.ds(pl.multiple_of(h * width, width), width)

    own = [
        pltpu.make_async_copy(q_hbm.at[0, :, head_cols(y, STACK)], qg.at[y], local_sem.at[0]),
        pltpu.make_async_copy(k_hbm.at[0, :, head_cols(y, D)], kvg.at[0, y, z], local_sem.at[1]),
        pltpu.make_async_copy(v_hbm.at[0, :, head_cols(y, D)], kvg.at[1, y, z], local_sem.at[2]),
        pltpu.make_async_copy(table_hbm, table, local_sem.at[3]),
    ]
    for copy in own:
        copy.start()
    barrier = pltpu.get_barrier_semaphore()
    others = [across(d) for d in range(1, NX)] + [twin]
    for peer in others:
        pl.semaphore_signal(barrier, inc=1, device_id=peer, device_id_type=MESH)

    def greet(k, carry):
        pl.semaphore_signal(barrier, inc=1, device_id=(r, lax.rem(s + k, SEQ)), device_id_type=MESH)
        return carry

    lax.fori_loop(1, SEQ, greet, 0)

    for h in range(HEADS):
        cols = slice(h * D, (h + 1) * D)
        pkv[h] = jnp.concatenate([pk_ref[:, cols].astype(F32), pv_ref[:, cols].astype(F32)], axis=0).astype(BF16)
    pg[x, c, z, y] = pkv[y]

    order = [lax.rem(z + k + NZ, NZ) for k in (0, 1, -1, 2, -2, 3, -3, 4)]
    inside = lax.broadcasted_iota(jnp.int32, (ROWS, ROWS), 1) - lax.broadcasted_iota(jnp.int32, (ROWS, ROWS), 0)
    for k in range(NZ):
        causal[k // HALF, :, (k % HALF) * ROWS : (k % HALF + 1) * ROWS] = jnp.where(inside <= (z - order[k]) * ROWS, 0.0, NEG)

    own[3].wait()

    def pick(t, carry):
        row = ids_smem[0, t] // D
        picked[pl.ds(t, 1), :] = table[pl.ds(row, 1), :]
        return carry

    lax.fori_loop(0, ROWS, pick, 0)
    length = lengths_ref[0]
    lanes = lax.broadcasted_iota(jnp.int32, (1, ROWS), 1)
    sub = lax.broadcasted_iota(jnp.int32, (ROWS, ROWS), 0)
    lane = lax.broadcasted_iota(jnp.int32, (ROWS, ROWS), 1)
    as_row = lambda column, shift=0: jnp.sum(jnp.where(sub == lane + shift, column, 0.0), axis=0, keepdims=True)
    as_column = lambda row: jnp.sum(jnp.where(sub == lane, row, 0), axis=1, keepdims=True)
    place = s * ROWS + lanes
    live = place < length
    spot = as_column(ids_ref[...] % D)
    reference = as_row(jnp.sum(jnp.where(lane == spot, picked[...], 0.0), axis=1, keepdims=True))
    rewards = jnp.where(live, -KL_BETA * (logp_ref[...] - reference), 0.0)
    rewards = rewards + jnp.where(place == length - 1, scores_ref[0], 0.0)
    rate = -1.0 / jnp.full((1, 1), horizon_ref[0], F32)
    gamma = jnp.exp(lanes.astype(F32) * rate)
    pl.semaphore_wait(barrier, len(others) + SEQ - 1)

    sent = []

    def prompt_copy(k):
        to = lax.rem(s + k, SEQ)
        return pltpu.make_async_remote_copy(
            src_ref=pkv.at[to // NZ], dst_ref=pg.at[x, c, z, y], send_sem=p_send.at[k - 1], recv_sem=p_recv.at[k - 1],
            device_id=(r, to), device_id_type=MESH,
        )

    def packet_copy(k):
        return pltpu.make_async_remote_copy(
            src_ref=packet, dst_ref=packets.at[z, y], send_sem=g_send.at[k - 1], recv_sem=g_recv.at[k - 1],
            device_id=(r, lax.rem(s + k, SEQ)), device_id_type=MESH,
        )

    def to_all(act):
        def step(k, carry):
            act(k)
            return carry

        lax.fori_loop(1, SEQ, step, 0)

    to_all(lambda k: prompt_copy(k).start())
    k_y, q_y = [], {}
    for d in range(1, NY):
        to = lax.rem(y + d, NY)
        for i, src in enumerate((k_hbm, v_hbm)):
            k_y.append(
                remote(
                    src.at[0, :, head_cols(to, D)], kvg.at[i, y, z],
                    ky_send.at[d - 1, i], ky_recv.at[d - 1, i], ahead(d),
                )
            )

    def send_queries(d):
        to = lax.rem(y + d, NY)
        q_y[d] = remote(q_hbm.at[0, :, head_cols(to, STACK)], qg.at[y], qy_send.at[d - 1], qy_recv.at[d - 1], ahead(d))

    send_queries(1)
    send_queries(3)

    to_all(lambda k: prompt_copy(k).wait_recv())
    p_x = {d: remote(pg.at[x, c], pg.at[x, c], px_send.at[d - 1], px_recv.at[d - 1], across(d)) for d in (1, 3)}
    p_c = {0: remote(pg.at[x, c], pg.at[x, c], pc_send.at[0], pc_recv.at[0], twin)}
    for copy in own[1:3]:
        copy.wait()
    for copy in k_y:
        copy.wait_recv()

    def ring_step(step):
        back = lax.rem(z - step + NZ, NZ)
        fore = lax.rem(z + step, NZ)
        if step < NZ // 2 - 1:
            parts = (kvg.at[:, :, back], kvg.at[:, :, fore])
        else:
            parts = (kvg.at[0, :, back], kvg.at[1, :, fore])
        out = [
            remote(parts[0], parts[0], ring_send.at[step, 0], ring_recv.at[step, 0], along(1)),
            remote(parts[1], parts[1], ring_send.at[step, 1], ring_recv.at[step, 1], along(NZ - 1)),
        ]
        sent.extend(out)
        return out

    ring = ring_step(0)

    def pass_over(d):
        src = lax.rem(x - d + NX, NX)
        p_c[d] = remote(pg.at[src, c], pg.at[src, c], pc_send.at[d], pc_recv.at[d], twin)

    def unpack(chunk, half, d, core):
        both = pg[lax.rem(x - d + NX, NX), core].astype(F32).reshape(SEQ, 16, D)
        rows = slice(half * SHARE, (half + 1) * SHARE)
        pk_all[chunk, rows] = both[:, :8, :].reshape(SHARE, D).astype(BF16)
        pv_all[chunk, rows] = both[:, 8:, :].reshape(SHARE, D).astype(BF16)

    def prompt_fold(i, d, rows=slice(None), first=False):
        block = lax.rem(y - d + NY, NY)
        if first:
            state = (jnp.full((STACK, D), NEG, F32), jnp.zeros((STACK, D), F32), jnp.zeros((STACK, D), F32))
        else:
            state = (peak[block], total[block], acc[block])
        peak[block], total[block], acc[block] = fold(state, stacked(qg, block), pk_all[i, rows], pv_all[i, rows])

    def ring_on(step):
        for copy in ring:
            copy.wait_recv()
        return ring_step(step)

    near = (0, 1, 3)
    unpack(0, 0, 0, c)
    for d in near:
        if d == 0:
            own[0].wait()
        else:
            q_y[d].wait_recv()
        prompt_fold(0, d, slice(0, SHARE), True)
    send_queries(2)
    p_c[0].wait_recv()
    unpack(0, 1, 0, 1 - c)
    for d in near:
        prompt_fold(0, d, slice(SHARE, 2 * SHARE))
    for d in (1, 3):
        p_x[d].wait_recv()
    for d in (1, 3):
        pass_over(d)
    way = 1 + 2 * c
    relayed = lax.rem(x - way + NX, NX)
    p_x[2] = remote(pg.at[relayed, c], pg.at[relayed, c], px_send.at[1], px_recv.at[1], across(way))
    unpack(1, 0, 1, c)
    unpack(1, 1, 3, c)
    for d in near:
        prompt_fold(1, d)
    ring = ring_on(1)
    for d in (1, 3):
        p_c[d].wait_recv()
    unpack(2, 0, 1, 1 - c)
    unpack(2, 1, 3, 1 - c)
    prompt_fold(2, 0)
    p_x[2].wait_recv()
    pass_over(2)
    for d in (1, 3):
        prompt_fold(2, d)
    p_c[2].wait_recv()
    unpack(3, 0, 2, c)
    unpack(3, 1, 2, 1 - c)
    for d in near:
        prompt_fold(3, d)
    ring = ring_on(2)
    q_y[2].wait_recv()
    for i in range(PROMPT // CHUNK):
        prompt_fold(i, 2, first=i == 0)
    sent += k_y + list(q_y.values()) + list(p_x.values()) + list(p_c.values())

    def turn(t):
        return lax.rem(2 + t + t * (t - 1) // 2, NY)

    def reply_half(half):
        for sup in range(NY):
            for k in range(HALF):
                rows = slice(k * ROWS, (k + 1) * ROWS)
                zz = order[half * HALF + k]
                staged[0, sup, rows] = kvg[0, sup, zz]
                staged[1, sup, rows] = kvg[1, sup, zz]
                past[sup, :, rows] = jnp.where(sup * SUPER + zz * ROWS + lanes < length, 0.0, NEG)

        def run(block):
            q = stacked(qg, block)
            state = (peak[block], total[block], acc[block])
            for sup in range(block):
                state = fold(state, q, staged[0, sup], staged[1, sup], past[sup])
            state = fold(state, q, staged[0, block], staged[1, block], causal[half] + past[block])
            peak[block], total[block], acc[block] = state

        def step(t, carry):
            block = lax.rem(y + turn(t), NY)
            if half == 0:

                @pl.when(t == 2)
                def _():
                    for copy in ring:
                        copy.wait_recv()
                    for copy in last_step():
                        copy.start()

            lax.switch(block, [functools.partial(run, b) for b in range(NY)])
            if half == 1:
                out = (acc[block] / total[block]).astype(BF16)
                part = jnp.zeros((ROWS, D), F32)
                for j in range(GROUP):
                    mine = out[j * ROWS : (j + 1) * ROWS]
                    ob[t, :, j * D : (j + 1) * D] = mine
                    part = part + mine.astype(F32) * head_ref[y, j : j + 1, :]

                @pl.when(t == 0)
                def _():
                    for copy in far_home():
                        copy.start()

                @pl.when((t > 0) & (t < NY - 1))
                def _():
                    home(t).start()

                @pl.when(t == 2)
                def _():
                    far_home()[1].wait_recv()
                    relay_home().start()

                here = (block * NZ + z) * ROWS + lax.broadcasted_iota(jnp.int32, (ROWS, 1), 0)
                column = jnp.where(here < length, jnp.sum(part, axis=1, keepdims=True), 0.0)
                row = as_row(column)
                change = jnp.where((block * NZ + z) * ROWS + lanes < length, as_row(column, 1) - row, 0.0)
                change = change + jnp.where(block == y, rewards, 0.0)
                lead = jnp.sum(change * gamma, axis=1, keepdims=True)
                packet[pl.ds(block, 1), :] = jnp.where(lanes == 0, lead, jnp.where(lanes == 1, row[:, :1], 0.0))
            return carry

        lax.fori_loop(0, NY, step, 0)

    def last_step():
        back, fore = lax.rem(z + NZ - 3, NZ), lax.rem(z + 3, NZ)
        return [
            pltpu.make_async_remote_copy(
                src_ref=ref, dst_ref=ref, send_sem=ring_send.at[3, i], recv_sem=ring_recv.at[3, i],
                device_id=along(d), device_id_type=MESH,
            )
            for i, (ref, d) in enumerate(((kvg.at[0, :, back], 1), (kvg.at[1, :, fore], NZ - 1)))
        ]

    def home(t):
        return pltpu.make_async_remote_copy(
            src_ref=ob.at[t], dst_ref=og.at[y], send_sem=oy_send.at[t], recv_sem=oy_recv.at[t],
            device_id=ahead(turn(t)), device_id_type=MESH,
        )

    def far_home():
        return [
            pltpu.make_async_remote_copy(
                src_ref=ob.at[0, :, :WING], dst_ref=og.at[y, :, :WING], send_sem=oy_send.at[0], recv_sem=oy_recv.at[0],
                device_id=ahead(2), device_id_type=MESH,
            ),
            pltpu.make_async_remote_copy(
                src_ref=ob.at[0, :, WING:], dst_ref=relay, send_sem=oy_send.at[3], recv_sem=oy_recv.at[3],
                device_id=ahead(3), device_id_type=MESH,
            ),
        ]

    def relay_home():
        return pltpu.make_async_remote_copy(
            src_ref=relay, dst_ref=og.at[lax.rem(y + 1, NY), :, WING:], send_sem=oy_send.at[4], recv_sem=oy_recv.at[4],
            device_id=ahead(3), device_id_type=MESH,
        )

    packet[...] = jnp.zeros_like(packet)
    reply_half(0)
    for copy in last_step():
        copy.wait_recv()
    reply_half(1)
    packets[z, y] = packet[...]
    to_all(lambda k: packet_copy(k).start())
    og[y] = ob[NY - 1]
    for copy in (home(1), home(2), far_home()[0], relay_home()):
        copy.wait_recv()
    back_home = [
        pltpu.make_async_copy(og.at[h], attn_ref.at[0, :, h * STACK : (h + 1) * STACK], local_sem.at[4 + h])
        for h in range(HEADS)
    ]
    for copy in back_home:
        copy.start()

    value = jnp.zeros((ROWS, D), F32)
    for h in range(HEADS):
        for j in range(GROUP):
            value = value + og[h, :, j * D : (j + 1) * D].astype(F32) * head_ref[h, j : j + 1, :]
    value = jnp.sum(value, axis=1, keepdims=True)
    value = jnp.where(s * ROWS + lax.broadcasted_iota(jnp.int32, (ROWS, 1), 0) < length, value, 0.0)
    value_row = as_row(value)
    values_ref[...] = value_row
    deltas = jnp.where(live, rewards + as_row(value, 1) - value_row, 0.0)
    gap = (lane - sub).astype(F32)
    decay = jnp.where(gap >= 0.0, jnp.exp(jnp.maximum(gap, 0.0) * rate), 0.0)
    local_adv = as_row(jnp.sum(decay * deltas, axis=1, keepdims=True))
    to_all(lambda k: packet_copy(k).wait_recv())

    carry = jnp.zeros((1, 1), F32)
    beyond = jnp.zeros((1, 1), F32)
    heads = packets[:, 0] + packets[:, 1] + packets[:, 2] + packets[:, 3]
    for yy in range(NY):
        rows = heads[:, yy, :]
        far = (yy * NZ + lax.broadcasted_iota(jnp.int32, (NZ, 1), 0) - s - 1).astype(F32)
        adv_weight = jnp.where(far >= 0.0, jnp.exp(jnp.maximum(far, 0.0) * ROWS * rate), 0.0)
        value_weight = jnp.where(far >= 1.0, jnp.exp((jnp.maximum(far - 1.0, 0.0) * ROWS + (ROWS - 1)) * rate), 0.0)
        carry = carry + jnp.sum(adv_weight * rows[:, :1] + value_weight * rows[:, 1:2], axis=0, keepdims=True)
        beyond = beyond + jnp.sum(jnp.where(far == 0.0, rows[:, 1:2], 0.0), axis=0, keepdims=True)
    along_row = lanes.astype(F32)
    tail = jnp.exp((ROWS - 1 - along_row) * rate) * beyond + jnp.exp((ROWS - along_row) * rate) * carry
    adv_ref[...] = jnp.where(live, local_adv + tail, 0.0)

    for copy in back_home:
        copy.wait()
    for copy in sent + last_step() + far_home() + [relay_home(), home(1), home(2)]:
        copy.wait_send()
    to_all(lambda k: prompt_copy(k).wait_send())
    to_all(lambda k: packet_copy(k).wait_send())


def local(queries, resp_keys, response_values, prompt_keys, prompt_values, value_head, token_ids, logprobs, ref_table, scores, lengths, horizon):
    smem = pl.BlockSpec(memory_space=pltpu.SMEM)
    vmem = pl.BlockSpec(memory_space=pltpu.VMEM)
    hbm = pl.BlockSpec(memory_space=pl.ANY)
    dma = pltpu.SemaphoreType.DMA
    return pl.pallas_call(
        body,
        out_shape=(
            jax.ShapeDtypeStruct((1, ROWS, HEADS * STACK), BF16),
            jax.ShapeDtypeStruct((1, ROWS), F32),
            jax.ShapeDtypeStruct((1, ROWS), F32),
        ),
        in_specs=[smem, smem, smem, smem, hbm, hbm, hbm, vmem, vmem, vmem, vmem, vmem, hbm],
        out_specs=(hbm, vmem, vmem),
        scratch_shapes=[
            pltpu.VMEM((NY, ROWS, STACK), BF16),
            pltpu.VMEM((2, NY, NZ, ROWS, D), BF16),
            pltpu.VMEM((HEADS, 16, D), BF16),
            pltpu.VMEM((NX, 2, NZ, NY, 16, D), BF16),
            pltpu.VMEM((PROMPT // CHUNK, CHUNK, D), BF16),
            pltpu.VMEM((PROMPT // CHUNK, CHUNK, D), BF16),
            pltpu.VMEM((NY, STACK, D), F32),
            pltpu.VMEM((NY, STACK, D), F32),
            pltpu.VMEM((NY, STACK, D), F32),
            pltpu.VMEM((2, NY, CHUNK, D), BF16),
            pltpu.VMEM((NY, 1, CHUNK), F32),
            pltpu.VMEM((2, ROWS, CHUNK), F32),
            pltpu.VMEM((NY, ROWS, STACK), BF16),
            pltpu.VMEM((HEADS, ROWS, STACK), BF16),
            pltpu.VMEM((VOCAB // D, D), F32),
            pltpu.VMEM((ROWS, D), F32),
            pltpu.VMEM((8, ROWS), F32),
            pltpu.VMEM((NZ, NY, 8, ROWS), F32),
            pltpu.VMEM((ROWS, WING), BF16),
            dma((8,)),
            dma((NY - 1,)), dma((NY - 1,)),
            dma((NY - 1, 2)), dma((NY - 1, 2)),
            dma((SEQ - 1,)), dma((SEQ - 1,)),
            dma((NX - 1,)), dma((NX - 1,)),
            dma((NX,)), dma((NX,)),
            dma((NZ // 2, 2)), dma((NZ // 2, 2)),
            dma((5,)), dma((5,)),
            dma((SEQ - 1,)), dma((SEQ - 1,)),
        ],
        compiler_params=pltpu.CompilerParams(
            collective_id=0, has_side_effects=True, vmem_limit_bytes=56 * 2**20
        ),
    )(
        scores, lengths, horizon, token_ids, queries, resp_keys, response_values, prompt_keys, prompt_values,
        value_head.reshape(HEADS, GROUP, D), token_ids, logprobs, ref_table.reshape(VOCAB // D, D),
    )


def solution(mesh):
    return jax.shard_map(
        local,
        mesh=mesh,
        in_specs=(
            P("resp", "seq", None),
            P("resp", "seq", None),
            P("resp", "seq", None),
            P(("resp", "seq"), None),
            P(("resp", "seq"), None),
            P(),
            P("resp", "seq"),
            P("resp", "seq"),
            P(),
            P("resp"),
            P("resp"),
            P("resp"),
        ),
        out_specs=(P("resp", "seq", None), P("resp", "seq"), P("resp", "seq")),
        check_vma=False,
    )
```

```python
import functools
import math

import jax
import jax.numpy as jnp
from jax import lax
from jax.experimental import pallas as pl
from jax.experimental.pallas import tpu as pltpu
from jax.sharding import PartitionSpec as P

F32 = jnp.float32
BF16 = jnp.bfloat16
MESH = pl.DeviceIdType.MESH

HEADS = 4
GROUP = 8
D = 128
NX, NY, NZ = 4, 4, 8
SEQ = NY * NZ
ROWS = 128
STACK = GROUP * ROWS
PROMPT = 2048
REPLY = 4096
SUPER = NZ * ROWS
HALF = NZ // 2
CHUNK = 512
SHARE = 256
WING = STACK // 2
VOCAB = 128256
KL_BETA = 0.01
NEG = -1e30
SCALE = math.log2(math.e) / math.sqrt(D)


def fold(state, q, k, v, bias=None):
    peak, total, acc = state
    s = lax.dot_general(q, k, (((1,), (1,)), ((), ())), preferred_element_type=F32)
    if bias is not None:
        s = (s.reshape(GROUP, ROWS, -1) + bias[None]).reshape(s.shape)
    new = jnp.maximum(peak, jnp.max(s, axis=1, keepdims=True))
    w = jnp.exp2((s - jnp.concatenate([new] * (s.shape[1] // D), axis=1)) * SCALE)
    shrink = jnp.exp2((peak - new) * SCALE)
    total = total * shrink + jnp.sum(w, axis=1, keepdims=True)
    acc = acc * shrink + jnp.dot(w.astype(BF16), v, preferred_element_type=F32)
    return new, total, acc


def stacked(qg, block):
    return jnp.concatenate([qg[block, :, j * D : (j + 1) * D] for j in range(GROUP)], axis=0)


def body(
    scores_ref, lengths_ref, horizon_ref, ids_smem, q_hbm, k_hbm, v_hbm, pk_ref, pv_ref, head_ref, ids_ref, logp_ref, table_hbm,
    attn_ref, values_ref, adv_ref,
    qg, kvg, pkv, pg, pk_all, pv_all, acc, peak, total, staged, past, causal, ob, og, table, picked, packet, packets,
    relay, spare_p, spare_g, local_sem, qy_send, qy_recv, ky_send, ky_recv, p_send, p_recv, px_send, px_recv,
    pc_send, pc_recv, ring_send, ring_recv, oy_send, oy_recv, g_send, g_recv,
):
    r = lax.axis_index("resp")
    s = lax.axis_index("seq")
    x, c = r // 2, r % 2
    y, z = s // NZ, s % NZ
    ahead = lambda d: (r, lax.rem(y + d, NY) * NZ + z)
    along = lambda d: (r, y * NZ + lax.rem(z + d, NZ))
    across = lambda d: (lax.rem(x + d, NX) * 2 + c, s)
    twin = (x * 2 + (1 - c), s)

    def remote(src, dst, send, recv, device):
        copy = pltpu.make_async_remote_copy(
            src_ref=src, dst_ref=dst, send_sem=send, recv_sem=recv, device_id=device, device_id_type=MESH
        )
        copy.start()
        return copy

    def head_cols(h, width):
        return pl.ds(pl.multiple_of(h * width, width), width)

    own = [
        pltpu.make_async_copy(q_hbm.at[0, :, head_cols(y, STACK)], qg.at[y], local_sem.at[0]),
        pltpu.make_async_copy(k_hbm.at[0, :, head_cols(y, D)], kvg.at[0, y, z], local_sem.at[1]),
        pltpu.make_async_copy(v_hbm.at[0, :, head_cols(y, D)], kvg.at[1, y, z], local_sem.at[2]),
        pltpu.make_async_copy(table_hbm, table, local_sem.at[3]),
    ]
    for copy in own:
        copy.start()
    barrier = pltpu.get_barrier_semaphore()
    others = [across(d) for d in range(1, NX)] + [twin]
    for peer in others:
        pl.semaphore_signal(barrier, inc=1, device_id=peer, device_id_type=MESH)

    def greet(k, carry):
        pl.semaphore_signal(barrier, inc=1, device_id=(r, lax.rem(s + k, SEQ)), device_id_type=MESH)
        return carry

    lax.fori_loop(1, SEQ, greet, 0)

    for h in range(HEADS):
        cols = slice(h * D, (h + 1) * D)
        pkv[h] = jnp.concatenate([pk_ref[:, cols].astype(F32), pv_ref[:, cols].astype(F32)], axis=0).astype(BF16)

    pl.semaphore_wait(barrier, len(others) + SEQ - 1)

    sent = []

    def prompt_copy(k):
        to = lax.rem(s + k, SEQ)
        return pltpu.make_async_remote_copy(
            src_ref=pkv.at[to // NZ], dst_ref=pg.at[x, c, z, y], send_sem=p_send, recv_sem=p_recv,
            device_id=(r, to), device_id_type=MESH,
        )

    def packet_copy(k):
        return pltpu.make_async_remote_copy(
            src_ref=packet, dst_ref=packets.at[z, y], send_sem=g_send, recv_sem=g_recv,
            device_id=(r, lax.rem(s + k, SEQ)), device_id_type=MESH,
        )

    def to_all(act):
        def step(k, carry):
            act(k)
            return carry

        lax.fori_loop(1, SEQ, step, 0)

    to_all(lambda k: prompt_copy(k).start())
    pltpu.make_async_copy(pkv.at[y], pg.at[x, c, z, y], p_recv).start()
    pltpu.make_async_copy(pkv.at[y], spare_p.at[z, y], p_send).start()
    k_y, q_y = [], {}
    for d in range(1, NY):
        to = lax.rem(y + d, NY)
        for i, src in enumerate((k_hbm, v_hbm)):
            k_y.append(
                remote(
                    src.at[0, :, head_cols(to, D)], kvg.at[i, y, z],
                    ky_send.at[d - 1, i], ky_recv.at[d - 1, i], ahead(d),
                )
            )

    def send_queries(d):
        to = lax.rem(y + d, NY)
        q_y[d] = remote(q_hbm.at[0, :, head_cols(to, STACK)], qg.at[y], qy_send.at[d - 1], qy_recv.at[d - 1], ahead(d))

    send_queries(1)
    send_queries(3)

    order = [lax.rem(z + k + NZ, NZ) for k in (0, 1, -1, 2, -2, 3, -3, 4)]
    inside = lax.broadcasted_iota(jnp.int32, (ROWS, ROWS), 1) - lax.broadcasted_iota(jnp.int32, (ROWS, ROWS), 0)
    for k in range(NZ):
        causal[k // HALF, :, (k % HALF) * ROWS : (k % HALF + 1) * ROWS] = jnp.where(inside <= (z - order[k]) * ROWS, 0.0, NEG)

    own[3].wait()

    def pick(t, carry):
        row = ids_smem[0, t] // D
        picked[pl.ds(t, 1), :] = table[pl.ds(row, 1), :]
        return carry

    lax.fori_loop(0, ROWS, pick, 0)
    length = lengths_ref[0]
    lanes = lax.broadcasted_iota(jnp.int32, (1, ROWS), 1)
    sub = lax.broadcasted_iota(jnp.int32, (ROWS, ROWS), 0)
    lane = lax.broadcasted_iota(jnp.int32, (ROWS, ROWS), 1)
    as_row = lambda column, shift=0: jnp.sum(jnp.where(sub == lane + shift, column, 0.0), axis=0, keepdims=True)
    as_column = lambda row: jnp.sum(jnp.where(sub == lane, row, 0), axis=1, keepdims=True)
    place = s * ROWS + lanes
    live = place < length
    spot = as_column(ids_ref[...] % D)
    reference = as_row(jnp.sum(jnp.where(lane == spot, picked[...], 0.0), axis=1, keepdims=True))
    rewards = jnp.where(live, -KL_BETA * (logp_ref[...] - reference), 0.0)
    rewards = rewards + jnp.where(place == length - 1, scores_ref[0], 0.0)
    rate = -1.0 / jnp.full((1, 1), horizon_ref[0], F32)
    gamma = jnp.exp(lanes.astype(F32) * rate)
    pltpu.make_async_copy(spare_p, pg.at[x, c], p_recv).wait()
    p_x = {d: remote(pg.at[x, c], pg.at[x, c], px_send.at[d - 1], px_recv.at[d - 1], across(d)) for d in (1, 3)}
    p_c = {0: remote(pg.at[x, c], pg.at[x, c], pc_send.at[0], pc_recv.at[0], twin)}
    for copy in own[1:3]:
        copy.wait()
    for copy in k_y:
        copy.wait_recv()

    def ring_step(step):
        back = lax.rem(z - step + NZ, NZ)
        fore = lax.rem(z + step, NZ)
        if step < NZ // 2 - 1:
            parts = (kvg.at[:, :, back], kvg.at[:, :, fore])
        else:
            parts = (kvg.at[0, :, back], kvg.at[1, :, fore])
        out = [
            remote(parts[0], parts[0], ring_send.at[step, 0], ring_recv.at[step, 0], along(1)),
            remote(parts[1], parts[1], ring_send.at[step, 1], ring_recv.at[step, 1], along(NZ - 1)),
        ]
        sent.extend(out)
        return out

    ring = ring_step(0)

    def pass_over(d):
        src = lax.rem(x - d + NX, NX)
        p_c[d] = remote(pg.at[src, c], pg.at[src, c], pc_send.at[d], pc_recv.at[d], twin)

    def unpack(chunk, half, d, core):
        both = pg[lax.rem(x - d + NX, NX), core].astype(F32).reshape(SEQ, 16, D)
        rows = slice(half * SHARE, (half + 1) * SHARE)
        pk_all[chunk, rows] = both[:, :8, :].reshape(SHARE, D).astype(BF16)
        pv_all[chunk, rows] = both[:, 8:, :].reshape(SHARE, D).astype(BF16)

    def prompt_fold(i, d, rows=slice(None), first=False):
        block = lax.rem(y - d + NY, NY)
        if first:
            state = (jnp.full((STACK, D), NEG, F32), jnp.zeros((STACK, D), F32), jnp.zeros((STACK, D), F32))
        else:
            state = (peak[block], total[block], acc[block])
        peak[block], total[block], acc[block] = fold(state, stacked(qg, block), pk_all[i, rows], pv_all[i, rows])

    def ring_on(step):
        for copy in ring:
            copy.wait_recv()
        return ring_step(step)

    near = (0, 1, 3)
    unpack(0, 0, 0, c)
    for d in near:
        if d == 0:
            own[0].wait()
        else:
            q_y[d].wait_recv()
        prompt_fold(0, d, slice(0, SHARE), True)
    send_queries(2)
    p_c[0].wait_recv()
    unpack(0, 1, 0, 1 - c)
    for d in near:
        prompt_fold(0, d, slice(SHARE, 2 * SHARE))
    for d in (1, 3):
        p_x[d].wait_recv()
    for d in (1, 3):
        pass_over(d)
    way = 1 + 2 * c
    relayed = lax.rem(x - way + NX, NX)
    p_x[2] = remote(pg.at[relayed, c], pg.at[relayed, c], px_send.at[1], px_recv.at[1], across(way))
    unpack(1, 0, 1, c)
    unpack(1, 1, 3, c)
    for d in near:
        prompt_fold(1, d)
    ring = ring_on(1)
    for d in (1, 3):
        p_c[d].wait_recv()
    unpack(2, 0, 1, 1 - c)
    unpack(2, 1, 3, 1 - c)
    prompt_fold(2, 0)
    p_x[2].wait_recv()
    pass_over(2)
    for d in (1, 3):
        prompt_fold(2, d)
    p_c[2].wait_recv()
    unpack(3, 0, 2, c)
    unpack(3, 1, 2, 1 - c)
    for d in near:
        prompt_fold(3, d)
    ring = ring_on(2)
    q_y[2].wait_recv()
    for i in range(PROMPT // CHUNK):
        prompt_fold(i, 2, first=i == 0)
    sent += k_y + list(q_y.values()) + list(p_x.values()) + list(p_c.values())

    def turn(t):
        return lax.rem(2 + t + t * (t - 1) // 2, NY)

    def reply_half(half):
        for sup in range(NY):
            for k in range(HALF):
                rows = slice(k * ROWS, (k + 1) * ROWS)
                zz = order[half * HALF + k]
                staged[0, sup, rows] = kvg[0, sup, zz]
                staged[1, sup, rows] = kvg[1, sup, zz]
                past[sup, :, rows] = jnp.where(sup * SUPER + zz * ROWS + lanes < length, 0.0, NEG)

        def run(block):
            q = stacked(qg, block)
            state = (peak[block], total[block], acc[block])
            for sup in range(block):
                state = fold(state, q, staged[0, sup], staged[1, sup], past[sup])
            state = fold(state, q, staged[0, block], staged[1, block], causal[half] + past[block])
            peak[block], total[block], acc[block] = state

        def step(t, carry):
            block = lax.rem(y + turn(t), NY)
            if half == 0:

                @pl.when(t == 2)
                def _():
                    for copy in ring:
                        copy.wait_recv()
                    for copy in last_step():
                        copy.start()

            lax.switch(block, [functools.partial(run, b) for b in range(NY)])
            if half == 1:
                out = (acc[block] / total[block]).astype(BF16)
                part = jnp.zeros((ROWS, D), F32)
                for j in range(GROUP):
                    mine = out[j * ROWS : (j + 1) * ROWS]
                    ob[t, :, j * D : (j + 1) * D] = mine
                    part = part + mine.astype(F32) * head_ref[y, j : j + 1, :]

                @pl.when(t == 0)
                def _():
                    for copy in far_home():
                        copy.start()

                @pl.when((t > 0) & (t < NY - 1))
                def _():
                    home(t).start()

                @pl.when(t == 2)
                def _():
                    far_home()[1].wait_recv()
                    relay_home().start()

                here = (block * NZ + z) * ROWS + lax.broadcasted_iota(jnp.int32, (ROWS, 1), 0)
                column = jnp.where(here < length, jnp.sum(part, axis=1, keepdims=True), 0.0)
                row = as_row(column)
                change = jnp.where((block * NZ + z) * ROWS + lanes < length, as_row(column, 1) - row, 0.0)
                change = change + jnp.where(block == y, rewards, 0.0)
                lead = jnp.sum(change * gamma, axis=1, keepdims=True)
                packet[pl.ds(block, 1), :] = jnp.where(lanes == 0, lead, jnp.where(lanes == 1, row[:, :1], 0.0))
            return carry

        lax.fori_loop(0, NY, step, 0)

    def last_step():
        back, fore = lax.rem(z + NZ - 3, NZ), lax.rem(z + 3, NZ)
        return [
            pltpu.make_async_remote_copy(
                src_ref=ref, dst_ref=ref, send_sem=ring_send.at[3, i], recv_sem=ring_recv.at[3, i],
                device_id=along(d), device_id_type=MESH,
            )
            for i, (ref, d) in enumerate(((kvg.at[0, :, back], 1), (kvg.at[1, :, fore], NZ - 1)))
        ]

    def home(t):
        return pltpu.make_async_remote_copy(
            src_ref=ob.at[t], dst_ref=og.at[y], send_sem=oy_send.at[t], recv_sem=oy_recv.at[t],
            device_id=ahead(turn(t)), device_id_type=MESH,
        )

    def far_home():
        return [
            pltpu.make_async_remote_copy(
                src_ref=ob.at[0, :, :WING], dst_ref=og.at[y, :, :WING], send_sem=oy_send.at[0], recv_sem=oy_recv.at[0],
                device_id=ahead(2), device_id_type=MESH,
            ),
            pltpu.make_async_remote_copy(
                src_ref=ob.at[0, :, WING:], dst_ref=relay, send_sem=oy_send.at[3], recv_sem=oy_recv.at[3],
                device_id=ahead(3), device_id_type=MESH,
            ),
        ]

    def relay_home():
        return pltpu.make_async_remote_copy(
            src_ref=relay, dst_ref=og.at[lax.rem(y + 1, NY), :, WING:], send_sem=oy_send.at[4], recv_sem=oy_recv.at[4],
            device_id=ahead(3), device_id_type=MESH,
        )

    packet[...] = jnp.zeros_like(packet)
    reply_half(0)
    for copy in last_step():
        copy.wait_recv()
    reply_half(1)
    to_all(lambda k: packet_copy(k).start())
    pltpu.make_async_copy(packet, packets.at[z, y], g_recv).start()
    pltpu.make_async_copy(packet, spare_g.at[z, y], g_send).start()
    og[y] = ob[NY - 1]
    for copy in (home(1), home(2), far_home()[0], relay_home()):
        copy.wait_recv()
    back_home = [
        pltpu.make_async_copy(og.at[h], attn_ref.at[0, :, h * STACK : (h + 1) * STACK], local_sem.at[4 + h])
        for h in range(HEADS)
    ]
    for copy in back_home:
        copy.start()

    value = jnp.zeros((ROWS, D), F32)
    for h in range(HEADS):
        for j in range(GROUP):
            value = value + og[h, :, j * D : (j + 1) * D].astype(F32) * head_ref[h, j : j + 1, :]
    value = jnp.sum(value, axis=1, keepdims=True)
    value = jnp.where(s * ROWS + lax.broadcasted_iota(jnp.int32, (ROWS, 1), 0) < length, value, 0.0)
    value_row = as_row(value)
    values_ref[...] = value_row
    deltas = jnp.where(live, rewards + as_row(value, 1) - value_row, 0.0)
    gap = (lane - sub).astype(F32)
    decay = jnp.where(gap >= 0.0, jnp.exp(jnp.maximum(gap, 0.0) * rate), 0.0)
    local_adv = as_row(jnp.sum(decay * deltas, axis=1, keepdims=True))
    pltpu.make_async_copy(spare_g, packets, g_recv).wait()

    carry = jnp.zeros((1, 1), F32)
    beyond = jnp.zeros((1, 1), F32)
    heads = packets[:, 0] + packets[:, 1] + packets[:, 2] + packets[:, 3]
    for yy in range(NY):
        rows = heads[:, yy, :]
        far = (yy * NZ + lax.broadcasted_iota(jnp.int32, (NZ, 1), 0) - s - 1).astype(F32)
        adv_weight = jnp.where(far >= 0.0, jnp.exp(jnp.maximum(far, 0.0) * ROWS * rate), 0.0)
        value_weight = jnp.where(far >= 1.0, jnp.exp((jnp.maximum(far - 1.0, 0.0) * ROWS + (ROWS - 1)) * rate), 0.0)
        carry = carry + jnp.sum(adv_weight * rows[:, :1] + value_weight * rows[:, 1:2], axis=0, keepdims=True)
        beyond = beyond + jnp.sum(jnp.where(far == 0.0, rows[:, 1:2], 0.0), axis=0, keepdims=True)
    along_row = lanes.astype(F32)
    tail = jnp.exp((ROWS - 1 - along_row) * rate) * beyond + jnp.exp((ROWS - along_row) * rate) * carry
    adv_ref[...] = jnp.where(live, local_adv + tail, 0.0)

    for copy in back_home:
        copy.wait()
    for copy in sent + last_step() + far_home() + [relay_home(), home(1), home(2)]:
        copy.wait_send()
    pltpu.make_async_copy(pg.at[x, c], spare_p, p_send).wait()
    pltpu.make_async_copy(packets, spare_g, g_send).wait()


def local(queries, resp_keys, response_values, prompt_keys, prompt_values, value_head, token_ids, logprobs, ref_table, scores, lengths, horizon):
    smem = pl.BlockSpec(memory_space=pltpu.SMEM)
    vmem = pl.BlockSpec(memory_space=pltpu.VMEM)
    hbm = pl.BlockSpec(memory_space=pl.ANY)
    dma = pltpu.SemaphoreType.DMA
    return pl.pallas_call(
        body,
        out_shape=(
            jax.ShapeDtypeStruct((1, ROWS, HEADS * STACK), BF16),
            jax.ShapeDtypeStruct((1, ROWS), F32),
            jax.ShapeDtypeStruct((1, ROWS), F32),
        ),
        in_specs=[smem, smem, smem, smem, hbm, hbm, hbm, vmem, vmem, vmem, vmem, vmem, hbm],
        out_specs=(hbm, vmem, vmem),
        scratch_shapes=[
            pltpu.VMEM((NY, ROWS, STACK), BF16),
            pltpu.VMEM((2, NY, NZ, ROWS, D), BF16),
            pltpu.VMEM((HEADS, 16, D), BF16),
            pltpu.VMEM((NX, 2, NZ, NY, 16, D), BF16),
            pltpu.VMEM((PROMPT // CHUNK, CHUNK, D), BF16),
            pltpu.VMEM((PROMPT // CHUNK, CHUNK, D), BF16),
            pltpu.VMEM((NY, STACK, D), F32),
            pltpu.VMEM((NY, STACK, D), F32),
            pltpu.VMEM((NY, STACK, D), F32),
            pltpu.VMEM((2, NY, CHUNK, D), BF16),
            pltpu.VMEM((NY, 1, CHUNK), F32),
            pltpu.VMEM((2, ROWS, CHUNK), F32),
            pltpu.VMEM((NY, ROWS, STACK), BF16),
            pltpu.VMEM((HEADS, ROWS, STACK), BF16),
            pltpu.VMEM((VOCAB // D, D), F32),
            pltpu.VMEM((ROWS, D), F32),
            pltpu.VMEM((8, ROWS), F32),
            pltpu.VMEM((NZ, NY, 8, ROWS), F32),
            pltpu.VMEM((ROWS, WING), BF16),
            pltpu.VMEM((NZ, NY, 16, D), BF16),
            pltpu.VMEM((NZ, NY, 8, ROWS), F32),
            dma((8,)),
            dma((NY - 1,)), dma((NY - 1,)),
            dma((NY - 1, 2)), dma((NY - 1, 2)),
            dma, dma,
            dma((NX - 1,)), dma((NX - 1,)),
            dma((NX,)), dma((NX,)),
            dma((NZ // 2, 2)), dma((NZ // 2, 2)),
            dma((5,)), dma((5,)),
            dma, dma,
        ],
        compiler_params=pltpu.CompilerParams(
            collective_id=0, has_side_effects=True, vmem_limit_bytes=56 * 2**20
        ),
    )(
        scores, lengths, horizon, token_ids, queries, resp_keys, response_values, prompt_keys, prompt_values,
        value_head.reshape(HEADS, GROUP, D), token_ids, logprobs, ref_table.reshape(VOCAB // D, D),
    )


def solution(mesh):
    return jax.shard_map(
        local,
        mesh=mesh,
        in_specs=(
            P("resp", "seq", None),
            P("resp", "seq", None),
            P("resp", "seq", None),
            P(("resp", "seq"), None),
            P(("resp", "seq"), None),
            P(),
            P("resp", "seq"),
            P("resp", "seq"),
            P(),
            P("resp"),
            P("resp"),
            P("resp"),
        ),
        out_specs=(P("resp", "seq", None), P("resp", "seq"), P("resp", "seq")),
        check_vma=False,
    )
```

```python
import functools
import math

import jax
import jax.numpy as jnp
from jax import lax
from jax.experimental import pallas as pl
from jax.experimental.pallas import tpu as pltpu
from jax.sharding import PartitionSpec as P

F32 = jnp.float32
BF16 = jnp.bfloat16
MESH = pl.DeviceIdType.MESH

HEADS = 4
GROUP = 8
D = 128
NX, NY, NZ = 4, 4, 8
SEQ = NY * NZ
ROWS = 128
STACK = GROUP * ROWS
PROMPT = 2048
REPLY = 4096
SUPER = NZ * ROWS
HALF = NZ // 2
CHUNK = 512
SHARE = 256
WING = STACK // 2
VOCAB = 128256
KL_BETA = 0.01
NEG = -1e30
SCALE = math.log2(math.e) / math.sqrt(D)


def fold(state, q, k, v, bias=None):
    peak, total, acc = state
    s = lax.dot_general(q, k, (((1,), (1,)), ((), ())), preferred_element_type=F32)
    if bias is not None:
        s = (s.reshape(GROUP, ROWS, -1) + bias[None]).reshape(s.shape)
    new = jnp.maximum(peak, jnp.max(s, axis=1, keepdims=True))
    w = jnp.exp2((s - jnp.concatenate([new] * (s.shape[1] // D), axis=1)) * SCALE)
    shrink = jnp.exp2((peak - new) * SCALE)
    total = total * shrink + jnp.sum(w, axis=1, keepdims=True)
    acc = acc * shrink + jnp.dot(w.astype(BF16), v, preferred_element_type=F32)
    return new, total, acc


def stacked(qg, block):
    return jnp.concatenate([qg[block, :, j * D : (j + 1) * D] for j in range(GROUP)], axis=0)


def body(
    scores_ref, lengths_ref, horizon_ref, ids_smem, q_hbm, k_hbm, v_hbm, pk_ref, pv_ref, head_ref, ids_ref, logp_ref, table_hbm,
    heads_ref, values_ref, adv_ref,
    qg, kvg, pkv, pg, pk_all, pv_all, acc, peak, total, staged, past, causal, ob, og, table, picked, packet, packets,
    relay, spare_p, spare_g, local_sem, qy_send, qy_recv, ky_send, ky_recv, p_send, p_recv, px_send, px_recv,
    pc_send, pc_recv, ring_send, ring_recv, oy_send, oy_recv, g_send, g_recv,
):
    r = lax.axis_index("resp")
    s = lax.axis_index("seq")
    x, c = r // 2, r % 2
    y, z = s // NZ, s % NZ
    ahead = lambda d: (r, lax.rem(y + d, NY) * NZ + z)
    along = lambda d: (r, y * NZ + lax.rem(z + d, NZ))
    across = lambda d: (lax.rem(x + d, NX) * 2 + c, s)
    twin = (x * 2 + (1 - c), s)

    def remote(src, dst, send, recv, device):
        copy = pltpu.make_async_remote_copy(
            src_ref=src, dst_ref=dst, send_sem=send, recv_sem=recv, device_id=device, device_id_type=MESH
        )
        copy.start()
        return copy

    def head_cols(h, width):
        return pl.ds(pl.multiple_of(h * width, width), width)

    own = [
        pltpu.make_async_copy(q_hbm.at[0, :, head_cols(y, STACK)], qg.at[y], local_sem.at[0]),
        pltpu.make_async_copy(k_hbm.at[0, :, head_cols(y, D)], kvg.at[0, y, z], local_sem.at[1]),
        pltpu.make_async_copy(v_hbm.at[0, :, head_cols(y, D)], kvg.at[1, y, z], local_sem.at[2]),
        pltpu.make_async_copy(table_hbm, table, local_sem.at[3]),
    ]
    for copy in own:
        copy.start()
    barrier = pltpu.get_barrier_semaphore()
    others = [across(d) for d in range(1, NX)] + [twin]
    for peer in others:
        pl.semaphore_signal(barrier, inc=1, device_id=peer, device_id_type=MESH)

    def greet(k, carry):
        pl.semaphore_signal(barrier, inc=1, device_id=(r, lax.rem(s + k, SEQ)), device_id_type=MESH)
        return carry

    lax.fori_loop(1, SEQ, greet, 0)

    for h in range(HEADS):
        cols = slice(h * D, (h + 1) * D)
        pkv[h] = jnp.concatenate([pk_ref[:, cols].astype(F32), pv_ref[:, cols].astype(F32)], axis=0).astype(BF16)

    pl.semaphore_wait(barrier, len(others) + SEQ - 1)

    sent = []

    def prompt_copy(k):
        to = lax.rem(s + k, SEQ)
        return pltpu.make_async_remote_copy(
            src_ref=pkv.at[to // NZ], dst_ref=pg.at[x, c, z, y], send_sem=p_send, recv_sem=p_recv,
            device_id=(r, to), device_id_type=MESH,
        )

    def packet_copy(k):
        return pltpu.make_async_remote_copy(
            src_ref=packet, dst_ref=packets.at[z, y], send_sem=g_send, recv_sem=g_recv,
            device_id=(r, lax.rem(s + k, SEQ)), device_id_type=MESH,
        )

    def to_all(act):
        def step(k, carry):
            act(k)
            return carry

        lax.fori_loop(1, SEQ, step, 0)

    to_all(lambda k: prompt_copy(k).start())
    pltpu.make_async_copy(pkv.at[y], pg.at[x, c, z, y], p_recv).start()
    pltpu.make_async_copy(pkv.at[y], spare_p.at[z, y], p_send).start()
    k_y, q_y = [], {}
    for d in range(1, NY):
        to = lax.rem(y + d, NY)
        for i, src in enumerate((k_hbm, v_hbm)):
            k_y.append(
                remote(
                    src.at[0, :, head_cols(to, D)], kvg.at[i, y, z],
                    ky_send.at[d - 1, i], ky_recv.at[d - 1, i], ahead(d),
                )
            )

    def send_queries(d):
        to = lax.rem(y + d, NY)
        q_y[d] = remote(q_hbm.at[0, :, head_cols(to, STACK)], qg.at[y], qy_send.at[d - 1], qy_recv.at[d - 1], ahead(d))

    send_queries(1)
    send_queries(3)

    order = [lax.rem(z + k + NZ, NZ) for k in (0, 1, -1, 2, -2, 3, -3, 4)]
    inside = lax.broadcasted_iota(jnp.int32, (ROWS, ROWS), 1) - lax.broadcasted_iota(jnp.int32, (ROWS, ROWS), 0)
    for k in range(NZ):
        causal[k // HALF, :, (k % HALF) * ROWS : (k % HALF + 1) * ROWS] = jnp.where(inside <= (z - order[k]) * ROWS, 0.0, NEG)

    own[3].wait()

    def pick(t, carry):
        row = ids_smem[0, t] // D
        picked[pl.ds(t, 1), :] = table[pl.ds(row, 1), :]
        return carry

    lax.fori_loop(0, ROWS, pick, 0)
    length = lengths_ref[0]
    lanes = lax.broadcasted_iota(jnp.int32, (1, ROWS), 1)
    sub = lax.broadcasted_iota(jnp.int32, (ROWS, ROWS), 0)
    lane = lax.broadcasted_iota(jnp.int32, (ROWS, ROWS), 1)
    as_row = lambda column, shift=0: jnp.sum(jnp.where(sub == lane + shift, column, 0.0), axis=0, keepdims=True)
    as_column = lambda row: jnp.sum(jnp.where(sub == lane, row, 0), axis=1, keepdims=True)
    place = s * ROWS + lanes
    live = place < length
    spot = as_column(ids_ref[...] % D)
    reference = as_row(jnp.sum(jnp.where(lane == spot, picked[...], 0.0), axis=1, keepdims=True))
    rewards = jnp.where(live, -KL_BETA * (logp_ref[...] - reference), 0.0)
    rewards = rewards + jnp.where(place == length - 1, scores_ref[0], 0.0)
    rate = -1.0 / jnp.full((1, 1), horizon_ref[0], F32)
    gamma = jnp.exp(lanes.astype(F32) * rate)
    pltpu.make_async_copy(spare_p, pg.at[x, c], p_recv).wait()
    p_x = {d: remote(pg.at[x, c], pg.at[x, c], px_send.at[d - 1], px_recv.at[d - 1], across(d)) for d in (1, 3)}
    p_c = {0: remote(pg.at[x, c], pg.at[x, c], pc_send.at[0], pc_recv.at[0], twin)}
    for copy in own[1:3]:
        copy.wait()
    for copy in k_y:
        copy.wait_recv()

    def ring_step(step):
        back = lax.rem(z - step + NZ, NZ)
        fore = lax.rem(z + step, NZ)
        if step < NZ // 2 - 1:
            parts = (kvg.at[:, :, back], kvg.at[:, :, fore])
        else:
            parts = (kvg.at[0, :, back], kvg.at[1, :, fore])
        out = [
            remote(parts[0], parts[0], ring_send.at[step, 0], ring_recv.at[step, 0], along(1)),
            remote(parts[1], parts[1], ring_send.at[step, 1], ring_recv.at[step, 1], along(NZ - 1)),
        ]
        sent.extend(out)
        return out

    ring = ring_step(0)

    def pass_over(d):
        src = lax.rem(x - d + NX, NX)
        p_c[d] = remote(pg.at[src, c], pg.at[src, c], pc_send.at[d], pc_recv.at[d], twin)

    def unpack(chunk, half, d, core):
        both = pg[lax.rem(x - d + NX, NX), core].astype(F32).reshape(SEQ, 16, D)
        rows = slice(half * SHARE, (half + 1) * SHARE)
        pk_all[chunk, rows] = both[:, :8, :].reshape(SHARE, D).astype(BF16)
        pv_all[chunk, rows] = both[:, 8:, :].reshape(SHARE, D).astype(BF16)

    def prompt_fold(d, *chunks, first=False):
        block = lax.rem(y - d + NY, NY)
        if first:
            state = (jnp.full((STACK, D), NEG, F32), jnp.zeros((STACK, D), F32), jnp.zeros((STACK, D), F32))
        else:
            state = (peak[block], total[block], acc[block])
        q = stacked(qg, block)
        for chunk in chunks:
            state = fold(state, q, pk_all[chunk], pv_all[chunk])
        peak[block], total[block], acc[block] = state

    def ring_on(step):
        for copy in ring:
            copy.wait_recv()
        return ring_step(step)

    unpack(0, 0, 0, c)
    own[0].wait()
    prompt_fold(0, (0, slice(0, SHARE)), first=True)
    p_c[0].wait_recv()
    unpack(0, 1, 0, 1 - c)
    prompt_fold(0, (0, slice(SHARE, 2 * SHARE)))
    for d in (1, 3):
        q_y[d].wait_recv()
    send_queries(2)
    for d in (1, 3):
        p_x[d].wait_recv()
    for d in (1, 3):
        pass_over(d)
    way = 1 + 2 * c
    relayed = lax.rem(x - way + NX, NX)
    p_x[2] = remote(pg.at[relayed, c], pg.at[relayed, c], px_send.at[1], px_recv.at[1], across(way))
    unpack(1, 0, 1, c)
    unpack(1, 1, 3, c)
    for d in (1, 3):
        prompt_fold(d, 0, 1, first=True)
    p_x[2].wait_recv()
    pass_over(2)
    prompt_fold(0, 1)
    ring = ring_on(1)
    for d in (1, 3):
        p_c[d].wait_recv()
    unpack(2, 0, 1, 1 - c)
    unpack(2, 1, 3, 1 - c)
    prompt_fold(0, 2)
    p_c[2].wait_recv()
    unpack(3, 0, 2, c)
    unpack(3, 1, 2, 1 - c)
    for d in (1, 3):
        prompt_fold(d, 2, 3)
    prompt_fold(0, 3)
    ring = ring_on(2)
    q_y[2].wait_recv()
    prompt_fold(2, *range(PROMPT // CHUNK), first=True)
    sent += k_y + list(q_y.values()) + list(p_x.values()) + list(p_c.values())

    def turn(t):
        return lax.rem(2 + t + t * (t - 1) // 2, NY)

    def reply_half(half):
        for sup in range(NY):
            for k in range(HALF):
                rows = slice(k * ROWS, (k + 1) * ROWS)
                zz = order[half * HALF + k]
                staged[0, sup, rows] = kvg[0, sup, zz]
                staged[1, sup, rows] = kvg[1, sup, zz]
                past[sup, :, rows] = jnp.where(sup * SUPER + zz * ROWS + lanes < length, 0.0, NEG)

        def run(block):
            q = stacked(qg, block)
            state = (peak[block], total[block], acc[block])
            for sup in range(block):
                state = fold(state, q, staged[0, sup], staged[1, sup], past[sup])
            state = fold(state, q, staged[0, block], staged[1, block], causal[half] + past[block])
            peak[block], total[block], acc[block] = state

        def step(t, carry):
            block = lax.rem(y + turn(t), NY)
            if half == 0:

                @pl.when(t == 2)
                def _():
                    for copy in ring:
                        copy.wait_recv()
                    for copy in last_step():
                        copy.start()

            lax.switch(block, [functools.partial(run, b) for b in range(NY)])
            if half == 1:
                out = (acc[block] / total[block]).astype(BF16)
                part = jnp.zeros((ROWS, D), F32)
                for j in range(GROUP):
                    mine = out[j * ROWS : (j + 1) * ROWS]
                    ob[t, :, j * D : (j + 1) * D] = mine
                    part = part + mine.astype(F32) * head_ref[y, j : j + 1, :]

                @pl.when(t == 0)
                def _():
                    for copy in far_home():
                        copy.start()

                @pl.when((t > 0) & (t < NY - 1))
                def _():
                    home(t).start()

                @pl.when(t == 2)
                def _():
                    far_home()[1].wait_recv()
                    relay_home().start()

                here = (block * NZ + z) * ROWS + lax.broadcasted_iota(jnp.int32, (ROWS, 1), 0)
                column = jnp.where(here < length, jnp.sum(part, axis=1, keepdims=True), 0.0)
                row = as_row(column)
                change = jnp.where((block * NZ + z) * ROWS + lanes < length, as_row(column, 1) - row, 0.0)
                change = change + jnp.where(block == y, rewards, 0.0)
                lead = jnp.sum(change * gamma, axis=1, keepdims=True)
                packet[pl.ds(block, 1), :] = jnp.where(lanes == 0, lead, jnp.where(lanes == 1, row[:, :1], 0.0))
            return carry

        lax.fori_loop(0, NY, step, 0)

    def last_step():
        back, fore = lax.rem(z + NZ - 3, NZ), lax.rem(z + 3, NZ)
        return [
            pltpu.make_async_remote_copy(
                src_ref=ref, dst_ref=ref, send_sem=ring_send.at[3, i], recv_sem=ring_recv.at[3, i],
                device_id=along(d), device_id_type=MESH,
            )
            for i, (ref, d) in enumerate(((kvg.at[0, :, back], 1), (kvg.at[1, :, fore], NZ - 1)))
        ]

    def home(t):
        return pltpu.make_async_remote_copy(
            src_ref=ob.at[t], dst_ref=og.at[y], send_sem=oy_send.at[t], recv_sem=oy_recv.at[t],
            device_id=ahead(turn(t)), device_id_type=MESH,
        )

    def far_home():
        return [
            pltpu.make_async_remote_copy(
                src_ref=ob.at[0, :, :WING], dst_ref=og.at[y, :, :WING], send_sem=oy_send.at[0], recv_sem=oy_recv.at[0],
                device_id=ahead(2), device_id_type=MESH,
            ),
            pltpu.make_async_remote_copy(
                src_ref=ob.at[0, :, WING:], dst_ref=relay, send_sem=oy_send.at[3], recv_sem=oy_recv.at[3],
                device_id=ahead(3), device_id_type=MESH,
            ),
        ]

    def relay_home():
        return pltpu.make_async_remote_copy(
            src_ref=relay, dst_ref=og.at[lax.rem(y + 1, NY), :, WING:], send_sem=oy_send.at[4], recv_sem=oy_recv.at[4],
            device_id=ahead(3), device_id_type=MESH,
        )

    packet[...] = jnp.zeros_like(packet)
    reply_half(0)
    for copy in last_step():
        copy.wait_recv()
    reply_half(1)
    to_all(lambda k: packet_copy(k).start())
    pltpu.make_async_copy(packet, packets.at[z, y], g_recv).start()
    pltpu.make_async_copy(packet, spare_g.at[z, y], g_send).start()
    og[y] = ob[NY - 1]
    for copy in (home(1), home(2), far_home()[0], relay_home()):
        copy.wait_recv()
    back_home = [
        pltpu.make_async_copy(og.at[h], heads_ref.at[h], local_sem.at[4 + h])
        for h in range(HEADS)
    ]
    for copy in back_home:
        copy.start()

    value = jnp.zeros((ROWS, D), F32)
    for h in range(HEADS):
        for j in range(GROUP):
            value = value + og[h, :, j * D : (j + 1) * D].astype(F32) * head_ref[h, j : j + 1, :]
    value = jnp.sum(value, axis=1, keepdims=True)
    value = jnp.where(s * ROWS + lax.broadcasted_iota(jnp.int32, (ROWS, 1), 0) < length, value, 0.0)
    value_row = as_row(value)
    values_ref[...] = value_row
    deltas = jnp.where(live, rewards + as_row(value, 1) - value_row, 0.0)
    gap = (lane - sub).astype(F32)
    decay = jnp.where(gap >= 0.0, jnp.exp(jnp.maximum(gap, 0.0) * rate), 0.0)
    local_adv = as_row(jnp.sum(decay * deltas, axis=1, keepdims=True))
    pltpu.make_async_copy(spare_g, packets, g_recv).wait()

    carry = jnp.zeros((1, 1), F32)
    beyond = jnp.zeros((1, 1), F32)
    heads = packets[:, 0] + packets[:, 1] + packets[:, 2] + packets[:, 3]
    for yy in range(NY):
        rows = heads[:, yy, :]
        far = (yy * NZ + lax.broadcasted_iota(jnp.int32, (NZ, 1), 0) - s - 1).astype(F32)
        adv_weight = jnp.where(far >= 0.0, jnp.exp(jnp.maximum(far, 0.0) * ROWS * rate), 0.0)
        value_weight = jnp.where(far >= 1.0, jnp.exp((jnp.maximum(far - 1.0, 0.0) * ROWS + (ROWS - 1)) * rate), 0.0)
        carry = carry + jnp.sum(adv_weight * rows[:, :1] + value_weight * rows[:, 1:2], axis=0, keepdims=True)
        beyond = beyond + jnp.sum(jnp.where(far == 0.0, rows[:, 1:2], 0.0), axis=0, keepdims=True)
    along_row = lanes.astype(F32)
    tail = jnp.exp((ROWS - 1 - along_row) * rate) * beyond + jnp.exp((ROWS - along_row) * rate) * carry
    adv_ref[...] = jnp.where(live, local_adv + tail, 0.0)

    for copy in back_home:
        copy.wait()
    for copy in sent + last_step() + far_home() + [relay_home(), home(1), home(2)]:
        copy.wait_send()
    pltpu.make_async_copy(pg.at[x, c], spare_p, p_send).wait()
    pltpu.make_async_copy(packets, spare_g, g_send).wait()


def local(queries, resp_keys, response_values, prompt_keys, prompt_values, value_head, token_ids, logprobs, ref_table, scores, lengths, horizon):
    smem = pl.BlockSpec(memory_space=pltpu.SMEM)
    vmem = pl.BlockSpec(memory_space=pltpu.VMEM)
    hbm = pl.BlockSpec(memory_space=pl.ANY)
    dma = pltpu.SemaphoreType.DMA
    heads, values, advantages = pl.pallas_call(
        body,
        out_shape=(
            jax.ShapeDtypeStruct((HEADS, ROWS, STACK), BF16),
            jax.ShapeDtypeStruct((1, ROWS), F32),
            jax.ShapeDtypeStruct((1, ROWS), F32),
        ),
        in_specs=[smem, smem, smem, smem, hbm, hbm, hbm, vmem, vmem, vmem, vmem, vmem, hbm],
        out_specs=(hbm, vmem, vmem),
        scratch_shapes=[
            pltpu.VMEM((NY, ROWS, STACK), BF16),
            pltpu.VMEM((2, NY, NZ, ROWS, D), BF16),
            pltpu.VMEM((HEADS, 16, D), BF16),
            pltpu.VMEM((NX, 2, NZ, NY, 16, D), BF16),
            pltpu.VMEM((PROMPT // CHUNK, CHUNK, D), BF16),
            pltpu.VMEM((PROMPT // CHUNK, CHUNK, D), BF16),
            pltpu.VMEM((NY, STACK, D), F32),
            pltpu.VMEM((NY, STACK, D), F32),
            pltpu.VMEM((NY, STACK, D), F32),
            pltpu.VMEM((2, NY, CHUNK, D), BF16),
            pltpu.VMEM((NY, 1, CHUNK), F32),
            pltpu.VMEM((2, ROWS, CHUNK), F32),
            pltpu.VMEM((NY, ROWS, STACK), BF16),
            pltpu.VMEM((HEADS, ROWS, STACK), BF16),
            pltpu.VMEM((VOCAB // D, D), F32),
            pltpu.VMEM((ROWS, D), F32),
            pltpu.VMEM((8, ROWS), F32),
            pltpu.VMEM((NZ, NY, 8, ROWS), F32),
            pltpu.VMEM((ROWS, WING), BF16),
            pltpu.VMEM((NZ, NY, 16, D), BF16),
            pltpu.VMEM((NZ, NY, 8, ROWS), F32),
            dma((8,)),
            dma((NY - 1,)), dma((NY - 1,)),
            dma((NY - 1, 2)), dma((NY - 1, 2)),
            dma, dma,
            dma((NX - 1,)), dma((NX - 1,)),
            dma((NX,)), dma((NX,)),
            dma((NZ // 2, 2)), dma((NZ // 2, 2)),
            dma((5,)), dma((5,)),
            dma, dma,
        ],
        compiler_params=pltpu.CompilerParams(
            collective_id=0, has_side_effects=True, vmem_limit_bytes=56 * 2**20
        ),
    )(
        scores, lengths, horizon, token_ids, queries, resp_keys, response_values, prompt_keys, prompt_values,
        value_head.reshape(HEADS, GROUP, D), token_ids, logprobs, ref_table.reshape(VOCAB // D, D),
    )
    return pl.pallas_call(
        gather_heads,
        out_shape=(
            jax.ShapeDtypeStruct((1, ROWS, HEADS * STACK), BF16),
            jax.ShapeDtypeStruct((1, ROWS), F32),
            jax.ShapeDtypeStruct((1, ROWS), F32),
        ),
        in_specs=[hbm, vmem, vmem],
        out_specs=(hbm, vmem, vmem),
        scratch_shapes=[dma((HEADS,))],
    )(heads, values, advantages)


def gather_heads(heads_ref, values_in, adv_in, attn_ref, values_ref, adv_ref, sem):
    copies = [
        pltpu.make_async_copy(heads_ref.at[h], attn_ref.at[0, :, h * STACK : (h + 1) * STACK], sem.at[h]) for h in range(HEADS)
    ]
    for copy in copies:
        copy.start()
    values_ref[...] = values_in[...]
    adv_ref[...] = adv_in[...]
    for copy in copies:
        copy.wait()


def solution(mesh):
    return jax.shard_map(
        local,
        mesh=mesh,
        in_specs=(
            P("resp", "seq", None),
            P("resp", "seq", None),
            P("resp", "seq", None),
            P(("resp", "seq"), None),
            P(("resp", "seq"), None),
            P(),
            P("resp", "seq"),
            P("resp", "seq"),
            P(),
            P("resp"),
            P("resp"),
            P("resp"),
        ),
        out_specs=(P("resp", "seq", None), P("resp", "seq"), P("resp", "seq")),
        check_vma=False,
    )
```

```python
import functools
import math

import jax
import jax.numpy as jnp
from jax import lax
from jax.experimental import pallas as pl
from jax.experimental.pallas import tpu as pltpu
from jax.sharding import PartitionSpec as P

F32 = jnp.float32
BF16 = jnp.bfloat16
MESH = pl.DeviceIdType.MESH

HEADS = 4
GROUP = 8
D = 128
NX, NY, NZ = 4, 4, 8
SEQ = NY * NZ
ROWS = 128
STACK = GROUP * ROWS
PROMPT = 2048
REPLY = 4096
SUPER = NZ * ROWS
HALF = NZ // 2
CHUNK = 512
SHARE = 256
WING = STACK // 2
VOCAB = 128256
KL_BETA = 0.01
NEG = -1e30
SCALE = math.log2(math.e) / math.sqrt(D)


def fold(state, q, k, v, bias=None):
    peak, total, acc = state
    s = lax.dot_general(q, k, (((1,), (1,)), ((), ())), preferred_element_type=F32)
    if bias is not None:
        s = (s.reshape(GROUP, ROWS, -1) + bias[None]).reshape(s.shape)
    new = jnp.maximum(peak, jnp.max(s, axis=1, keepdims=True))
    w = jnp.exp2((s - jnp.concatenate([new] * (s.shape[1] // D), axis=1)) * SCALE)
    shrink = jnp.exp2((peak - new) * SCALE)
    total = total * shrink + jnp.sum(w, axis=1, keepdims=True)
    acc = acc * shrink + jnp.dot(w.astype(BF16), v, preferred_element_type=F32)
    return new, total, acc


def stacked(qg, block):
    return jnp.concatenate([qg[block, :, j * D : (j + 1) * D] for j in range(GROUP)], axis=0)


def body(
    scores_ref, lengths_ref, horizon_ref, ids_smem, q_hbm, k_hbm, v_hbm, pk_ref, pv_ref, head_ref, ids_ref, logp_ref, table_hbm,
    heads_ref, values_ref, adv_ref,
    qg, kvg, pkv, pg, pk_all, pv_all, acc, peak, total, staged, past, causal, ob, og, table, picked, packet, packets,
    relay, spare_p, spare_g, local_sem, qy_send, qy_recv, ky_send, ky_recv, p_send, p_recv, px_send, px_recv,
    pc_send, pc_recv, ring_send, ring_recv, oy_send, oy_recv, g_send, g_recv,
):
    r = lax.axis_index("resp")
    s = lax.axis_index("seq")
    x, c = r // 2, r % 2
    y, z = s // NZ, s % NZ
    ahead = lambda d: (r, lax.rem(y + d, NY) * NZ + z)
    along = lambda d: (r, y * NZ + lax.rem(z + d, NZ))
    across = lambda d: (lax.rem(x + d, NX) * 2 + c, s)
    twin = (x * 2 + (1 - c), s)

    def remote(src, dst, send, recv, device):
        copy = pltpu.make_async_remote_copy(
            src_ref=src, dst_ref=dst, send_sem=send, recv_sem=recv, device_id=device, device_id_type=MESH
        )
        copy.start()
        return copy

    def head_cols(h, width):
        return pl.ds(pl.multiple_of(h * width, width), width)

    own = [
        pltpu.make_async_copy(q_hbm.at[0, :, head_cols(y, STACK)], qg.at[y], local_sem.at[0]),
        pltpu.make_async_copy(k_hbm.at[0, :, head_cols(y, D)], kvg.at[0, y, z], local_sem.at[1]),
        pltpu.make_async_copy(v_hbm.at[0, :, head_cols(y, D)], kvg.at[1, y, z], local_sem.at[2]),
        pltpu.make_async_copy(table_hbm, table, local_sem.at[3]),
    ]
    for copy in own:
        copy.start()
    barrier = pltpu.get_barrier_semaphore()
    others = [across(d) for d in range(1, NX)] + [twin]
    for peer in others:
        pl.semaphore_signal(barrier, inc=1, device_id=peer, device_id_type=MESH)

    def greet(k, carry):
        pl.semaphore_signal(barrier, inc=1, device_id=(r, lax.rem(s + k, SEQ)), device_id_type=MESH)
        return carry

    lax.fori_loop(1, SEQ, greet, 0)

    for h in range(HEADS):
        cols = slice(h * D, (h + 1) * D)
        pkv[h] = jnp.concatenate([pk_ref[:, cols].astype(F32), pv_ref[:, cols].astype(F32)], axis=0).astype(BF16)

    pl.semaphore_wait(barrier, len(others) + SEQ - 1)

    sent = []

    def prompt_copy(k):
        to = lax.rem(s + k, SEQ)
        return pltpu.make_async_remote_copy(
            src_ref=pkv.at[to // NZ], dst_ref=pg.at[x, c, z, y], send_sem=p_send, recv_sem=p_recv,
            device_id=(r, to), device_id_type=MESH,
        )

    def packet_copy(k):
        return pltpu.make_async_remote_copy(
            src_ref=packet, dst_ref=packets.at[z, y], send_sem=g_send, recv_sem=g_recv,
            device_id=(r, lax.rem(s + k, SEQ)), device_id_type=MESH,
        )

    def to_all(act):
        def step(k, carry):
            act(k)
            return carry

        lax.fori_loop(1, SEQ, step, 0)

    to_all(lambda k: prompt_copy(k).start())
    pltpu.make_async_copy(pkv.at[y], pg.at[x, c, z, y], p_recv).start()
    pltpu.make_async_copy(pkv.at[y], spare_p.at[z, y], p_send).start()
    k_y, q_y = [], {}
    for d in range(1, NY):
        to = lax.rem(y + d, NY)
        for i, src in enumerate((k_hbm, v_hbm)):
            k_y.append(
                remote(
                    src.at[0, :, head_cols(to, D)], kvg.at[i, y, z],
                    ky_send.at[d - 1, i], ky_recv.at[d - 1, i], ahead(d),
                )
            )

    def send_queries(d):
        to = lax.rem(y + d, NY)
        q_y[d] = remote(q_hbm.at[0, :, head_cols(to, STACK)], qg.at[y], qy_send.at[d - 1], qy_recv.at[d - 1], ahead(d))

    send_queries(1)
    send_queries(3)

    order = [lax.rem(z + k + NZ, NZ) for k in (0, 1, -1, 2, -2, 3, -3, 4)]
    inside = lax.broadcasted_iota(jnp.int32, (ROWS, ROWS), 1) - lax.broadcasted_iota(jnp.int32, (ROWS, ROWS), 0)
    for k in range(NZ):
        causal[k // HALF, :, (k % HALF) * ROWS : (k % HALF + 1) * ROWS] = jnp.where(inside <= (z - order[k]) * ROWS, 0.0, NEG)

    own[3].wait()

    def pick(t, carry):
        row = ids_smem[0, t] // D
        picked[pl.ds(t, 1), :] = table[pl.ds(row, 1), :]
        return carry

    lax.fori_loop(0, ROWS, pick, 0)
    length = lengths_ref[0]
    lanes = lax.broadcasted_iota(jnp.int32, (1, ROWS), 1)
    sub = lax.broadcasted_iota(jnp.int32, (ROWS, ROWS), 0)
    lane = lax.broadcasted_iota(jnp.int32, (ROWS, ROWS), 1)
    as_row = lambda column, shift=0: jnp.sum(jnp.where(sub == lane + shift, column, 0.0), axis=0, keepdims=True)
    as_column = lambda row: jnp.sum(jnp.where(sub == lane, row, 0), axis=1, keepdims=True)
    place = s * ROWS + lanes
    live = place < length
    spot = as_column(ids_ref[...] % D)
    reference = as_row(jnp.sum(jnp.where(lane == spot, picked[...], 0.0), axis=1, keepdims=True))
    rewards = jnp.where(live, -KL_BETA * (logp_ref[...] - reference), 0.0)
    rewards = rewards + jnp.where(place == length - 1, scores_ref[0], 0.0)
    rate = -1.0 / jnp.full((1, 1), horizon_ref[0], F32)
    gamma = jnp.exp(lanes.astype(F32) * rate)
    pltpu.make_async_copy(spare_p, pg.at[x, c], p_recv).wait()
    p_x = {d: remote(pg.at[x, c], pg.at[x, c], px_send.at[d - 1], px_recv.at[d - 1], across(d)) for d in (1, 3)}
    p_c = {0: remote(pg.at[x, c], pg.at[x, c], pc_send.at[0], pc_recv.at[0], twin)}
    for copy in own[1:3]:
        copy.wait()
    for copy in k_y:
        copy.wait_recv()

    def ring_step(step):
        back = lax.rem(z - step + NZ, NZ)
        fore = lax.rem(z + step, NZ)
        if step < NZ // 2 - 1:
            parts = (kvg.at[:, :, back], kvg.at[:, :, fore])
        else:
            parts = (kvg.at[0, :, back], kvg.at[1, :, fore])
        out = [
            remote(parts[0], parts[0], ring_send.at[step, 0], ring_recv.at[step, 0], along(1)),
            remote(parts[1], parts[1], ring_send.at[step, 1], ring_recv.at[step, 1], along(NZ - 1)),
        ]
        sent.extend(out)
        return out

    ring = ring_step(0)

    def pass_over(d):
        src = lax.rem(x - d + NX, NX)
        p_c[d] = remote(pg.at[src, c], pg.at[src, c], pc_send.at[d], pc_recv.at[d], twin)

    def unpack(chunk, half, d, core):
        both = pg[lax.rem(x - d + NX, NX), core].astype(F32).reshape(SEQ, 16, D)
        rows = slice(half * SHARE, (half + 1) * SHARE)
        pk_all[chunk, rows] = both[:, :8, :].reshape(SHARE, D).astype(BF16)
        pv_all[chunk, rows] = both[:, 8:, :].reshape(SHARE, D).astype(BF16)

    def prompt_fold(d, *chunks, first=False):
        block = lax.rem(y - d + NY, NY)
        if first:
            state = (jnp.full((STACK, D), NEG, F32), jnp.zeros((STACK, D), F32), jnp.zeros((STACK, D), F32))
        else:
            state = (peak[block], total[block], acc[block])
        q = stacked(qg, block)
        for chunk in chunks:
            state = fold(state, q, pk_all[chunk], pv_all[chunk])
        peak[block], total[block], acc[block] = state

    def ring_on(step):
        for copy in ring:
            copy.wait_recv()
        return ring_step(step)

    unpack(0, 0, 0, c)
    own[0].wait()
    prompt_fold(0, (0, slice(0, SHARE)), first=True)
    p_c[0].wait_recv()
    unpack(0, 1, 0, 1 - c)
    prompt_fold(0, (0, slice(SHARE, 2 * SHARE)))
    for d in (1, 3):
        q_y[d].wait_recv()
    send_queries(2)
    for d in (1, 3):
        p_x[d].wait_recv()
    for d in (1, 3):
        pass_over(d)
    way = 1 + 2 * c
    relayed = lax.rem(x - way + NX, NX)
    p_x[2] = remote(pg.at[relayed, c], pg.at[relayed, c], px_send.at[1], px_recv.at[1], across(way))
    unpack(1, 0, 1, c)
    unpack(1, 1, 3, c)
    for d in (1, 3):
        prompt_fold(d, 0, 1, first=True)
    p_x[2].wait_recv()
    pass_over(2)
    prompt_fold(0, 1)
    ring = ring_on(1)
    for d in (1, 3):
        p_c[d].wait_recv()
    unpack(2, 0, 1, 1 - c)
    unpack(2, 1, 3, 1 - c)
    prompt_fold(0, 2)
    p_c[2].wait_recv()
    unpack(3, 0, 2, c)
    unpack(3, 1, 2, 1 - c)
    for d in (1, 3):
        prompt_fold(d, 2, 3)
    prompt_fold(0, 3)
    ring = ring_on(2)
    q_y[2].wait_recv()
    prompt_fold(2, *range(PROMPT // CHUNK), first=True)
    sent += k_y + list(q_y.values()) + list(p_x.values()) + list(p_c.values())

    def turn(t):
        return lax.rem(2 + t + t * (t - 1) // 2, NY)

    def reply_half(half):
        for sup in range(NY):
            for k in range(HALF):
                rows = slice(k * ROWS, (k + 1) * ROWS)
                zz = order[half * HALF + k]
                staged[0, sup, rows] = kvg[0, sup, zz]
                staged[1, sup, rows] = kvg[1, sup, zz]
                past[sup, :, rows] = jnp.where(sup * SUPER + zz * ROWS + lanes < length, 0.0, NEG)

        def run(block):
            q = stacked(qg, block)
            state = (peak[block], total[block], acc[block])
            for sup in range(block):
                state = fold(state, q, staged[0, sup], staged[1, sup], past[sup])
            state = fold(state, q, staged[0, block], staged[1, block], causal[half] + past[block])
            peak[block], total[block], acc[block] = state

        def step(t, carry):
            block = lax.rem(y + turn(t), NY)
            if half == 0:

                @pl.when(t == 2)
                def _():
                    for copy in ring:
                        copy.wait_recv()
                    for copy in last_step():
                        copy.start()

            lax.switch(block, [functools.partial(run, b) for b in range(NY)])
            if half == 1:
                out = (acc[block] / total[block]).astype(BF16)
                part = jnp.zeros((ROWS, D), F32)
                for j in range(GROUP):
                    mine = out[j * ROWS : (j + 1) * ROWS]
                    ob[t, :, j * D : (j + 1) * D] = mine
                    part = part + mine.astype(F32) * head_ref[y, j : j + 1, :]

                @pl.when(t == 0)
                def _():
                    for copy in far_home():
                        copy.start()

                @pl.when((t > 0) & (t < NY - 1))
                def _():
                    home(t).start()

                @pl.when(t == 2)
                def _():
                    far_home()[1].wait_recv()
                    relay_home().start()

                here = (block * NZ + z) * ROWS + lax.broadcasted_iota(jnp.int32, (ROWS, 1), 0)
                column = jnp.where(here < length, jnp.sum(part, axis=1, keepdims=True), 0.0)
                row = as_row(column)
                change = jnp.where((block * NZ + z) * ROWS + lanes < length, as_row(column, 1) - row, 0.0)
                change = change + jnp.where(block == y, rewards, 0.0)
                lead = jnp.sum(change * gamma, axis=1, keepdims=True)
                packet[pl.ds(block, 1), :] = jnp.where(lanes == 0, lead, jnp.where(lanes == 1, row[:, :1], 0.0))
            return carry

        lax.fori_loop(0, NY, step, 0)

    def last_step():
        back, fore = lax.rem(z + NZ - 3, NZ), lax.rem(z + 3, NZ)
        return [
            pltpu.make_async_remote_copy(
                src_ref=ref, dst_ref=ref, send_sem=ring_send.at[3, i], recv_sem=ring_recv.at[3, i],
                device_id=along(d), device_id_type=MESH,
            )
            for i, (ref, d) in enumerate(((kvg.at[0, :, back], 1), (kvg.at[1, :, fore], NZ - 1)))
        ]

    def home(t):
        return pltpu.make_async_remote_copy(
            src_ref=ob.at[t], dst_ref=og.at[y], send_sem=oy_send.at[t], recv_sem=oy_recv.at[t],
            device_id=ahead(turn(t)), device_id_type=MESH,
        )

    def far_home():
        return [
            pltpu.make_async_remote_copy(
                src_ref=ob.at[0, :, :WING], dst_ref=og.at[y, :, :WING], send_sem=oy_send.at[0], recv_sem=oy_recv.at[0],
                device_id=ahead(2), device_id_type=MESH,
            ),
            pltpu.make_async_remote_copy(
                src_ref=ob.at[0, :, WING:], dst_ref=relay, send_sem=oy_send.at[3], recv_sem=oy_recv.at[3],
                device_id=ahead(3), device_id_type=MESH,
            ),
        ]

    def relay_home():
        return pltpu.make_async_remote_copy(
            src_ref=relay, dst_ref=og.at[lax.rem(y + 1, NY), :, WING:], send_sem=oy_send.at[4], recv_sem=oy_recv.at[4],
            device_id=ahead(3), device_id_type=MESH,
        )

    packet[...] = jnp.zeros_like(packet)
    reply_half(0)
    for copy in last_step():
        copy.wait_recv()
    reply_half(1)
    to_all(lambda k: packet_copy(k).start())
    pltpu.make_async_copy(packet, packets.at[z, y], g_recv).start()
    pltpu.make_async_copy(packet, spare_g.at[z, y], g_send).start()
    og[y] = ob[NY - 1]
    for copy in (home(1), home(2), far_home()[0], relay_home()):
        copy.wait_recv()
    back_home = [
        pltpu.make_async_copy(og.at[h], heads_ref.at[h], local_sem.at[4 + h])
        for h in range(HEADS)
    ]
    for copy in back_home:
        copy.start()

    value = jnp.zeros((ROWS, D), F32)
    for h in range(HEADS):
        for j in range(GROUP):
            value = value + og[h, :, j * D : (j + 1) * D].astype(F32) * head_ref[h, j : j + 1, :]
    value = jnp.sum(value, axis=1, keepdims=True)
    value = jnp.where(s * ROWS + lax.broadcasted_iota(jnp.int32, (ROWS, 1), 0) < length, value, 0.0)
    value_row = as_row(value)
    values_ref[...] = value_row
    deltas = jnp.where(live, rewards + as_row(value, 1) - value_row, 0.0)
    gap = (lane - sub).astype(F32)
    decay = jnp.where(gap >= 0.0, jnp.exp(jnp.maximum(gap, 0.0) * rate), 0.0)
    local_adv = as_row(jnp.sum(decay * deltas, axis=1, keepdims=True))
    pltpu.make_async_copy(spare_g, packets, g_recv).wait()

    carry = jnp.zeros((1, 1), F32)
    beyond = jnp.zeros((1, 1), F32)
    heads = packets[:, 0] + packets[:, 1] + packets[:, 2] + packets[:, 3]
    for yy in range(NY):
        rows = heads[:, yy, :]
        far = (yy * NZ + lax.broadcasted_iota(jnp.int32, (NZ, 1), 0) - s - 1).astype(F32)
        adv_weight = jnp.where(far >= 0.0, jnp.exp(jnp.maximum(far, 0.0) * ROWS * rate), 0.0)
        value_weight = jnp.where(far >= 1.0, jnp.exp((jnp.maximum(far - 1.0, 0.0) * ROWS + (ROWS - 1)) * rate), 0.0)
        carry = carry + jnp.sum(adv_weight * rows[:, :1] + value_weight * rows[:, 1:2], axis=0, keepdims=True)
        beyond = beyond + jnp.sum(jnp.where(far == 0.0, rows[:, 1:2], 0.0), axis=0, keepdims=True)
    along_row = lanes.astype(F32)
    tail = jnp.exp((ROWS - 1 - along_row) * rate) * beyond + jnp.exp((ROWS - along_row) * rate) * carry
    adv_ref[...] = jnp.where(live, local_adv + tail, 0.0)

    for copy in back_home:
        copy.wait()
    for copy in sent + last_step() + far_home() + [relay_home(), home(1), home(2)]:
        copy.wait_send()
    pltpu.make_async_copy(pg.at[x, c], spare_p, p_send).wait()
    pltpu.make_async_copy(packets, spare_g, g_send).wait()


def local(queries, resp_keys, response_values, prompt_keys, prompt_values, value_head, token_ids, logprobs, ref_table, scores, lengths, horizon):
    smem = pl.BlockSpec(memory_space=pltpu.SMEM)
    vmem = pl.BlockSpec(memory_space=pltpu.VMEM)
    hbm = pl.BlockSpec(memory_space=pl.ANY)
    dma = pltpu.SemaphoreType.DMA
    heads, values, advantages = pl.pallas_call(
        body,
        out_shape=(
            jax.ShapeDtypeStruct((HEADS, ROWS, STACK), BF16),
            jax.ShapeDtypeStruct((1, ROWS), F32),
            jax.ShapeDtypeStruct((1, ROWS), F32),
        ),
        in_specs=[smem, smem, smem, smem, hbm, hbm, hbm, vmem, vmem, vmem, vmem, vmem, hbm],
        out_specs=(hbm, vmem, vmem),
        scratch_shapes=[
            pltpu.VMEM((NY, ROWS, STACK), BF16),
            pltpu.VMEM((2, NY, NZ, ROWS, D), BF16),
            pltpu.VMEM((HEADS, 16, D), BF16),
            pltpu.VMEM((NX, 2, NZ, NY, 16, D), BF16),
            pltpu.VMEM((PROMPT // CHUNK, CHUNK, D), BF16),
            pltpu.VMEM((PROMPT // CHUNK, CHUNK, D), BF16),
            pltpu.VMEM((NY, STACK, D), F32),
            pltpu.VMEM((NY, STACK, D), F32),
            pltpu.VMEM((NY, STACK, D), F32),
            pltpu.VMEM((2, NY, CHUNK, D), BF16),
            pltpu.VMEM((NY, 1, CHUNK), F32),
            pltpu.VMEM((2, ROWS, CHUNK), F32),
            pltpu.VMEM((NY, ROWS, STACK), BF16),
            pltpu.VMEM((HEADS, ROWS, STACK), BF16),
            pltpu.VMEM((VOCAB // D, D), F32),
            pltpu.VMEM((ROWS, D), F32),
            pltpu.VMEM((8, ROWS), F32),
            pltpu.VMEM((NZ, NY, 8, ROWS), F32),
            pltpu.VMEM((ROWS, WING), BF16),
            pltpu.VMEM((NZ, NY, 16, D), BF16),
            pltpu.VMEM((NZ, NY, 8, ROWS), F32),
            dma((8,)),
            dma((NY - 1,)), dma((NY - 1,)),
            dma((NY - 1, 2)), dma((NY - 1, 2)),
            dma, dma,
            dma((NX - 1,)), dma((NX - 1,)),
            dma((NX,)), dma((NX,)),
            dma((NZ // 2, 2)), dma((NZ // 2, 2)),
            dma((5,)), dma((5,)),
            dma, dma,
        ],
        compiler_params=pltpu.CompilerParams(
            collective_id=0, has_side_effects=True, vmem_limit_bytes=56 * 2**20
        ),
    )(
        scores, lengths, horizon, token_ids, queries, resp_keys, response_values, prompt_keys, prompt_values,
        value_head.reshape(HEADS, GROUP, D), token_ids, logprobs, ref_table.reshape(VOCAB // D, D),
    )
    return pl.pallas_call(
        gather_heads,
        out_shape=(
            jax.ShapeDtypeStruct((1, ROWS, HEADS * STACK), BF16),
            jax.ShapeDtypeStruct((1, ROWS), F32),
            jax.ShapeDtypeStruct((1, ROWS), F32),
        ),
        in_specs=[vmem, vmem, vmem],
        out_specs=(vmem, vmem, vmem),
    )(heads, values, advantages)


def gather_heads(heads_ref, values_in, adv_in, attn_ref, values_ref, adv_ref):
    for h in range(HEADS):
        attn_ref[0, :, h * STACK : (h + 1) * STACK] = heads_ref[h]
    values_ref[...] = values_in[...]
    adv_ref[...] = adv_in[...]


def solution(mesh):
    return jax.shard_map(
        local,
        mesh=mesh,
        in_specs=(
            P("resp", "seq", None),
            P("resp", "seq", None),
            P("resp", "seq", None),
            P(("resp", "seq"), None),
            P(("resp", "seq"), None),
            P(),
            P("resp", "seq"),
            P("resp", "seq"),
            P(),
            P("resp"),
            P("resp"),
            P("resp"),
        ),
        out_specs=(P("resp", "seq", None), P("resp", "seq"), P("resp", "seq")),
        check_vma=False,
    )
```
